256 devices in a mesh: rows: 128 (over z, y, x), probe: 2 (over core).
Axes of the slice: x: 4, y: 4, z: 8, core: 2. Of those that a mesh axis runs over, the one named last changes fastest.
Arguments:
- probe_matrix: bfloat16 [256, 262144], P('probe', 'rows'), may hold values from -6 to 6
- near_blocks: bfloat16 [1024, 16, 256, 256], P('rows', 'probe'), may hold values from -0.01171875 to 0.01171875
- block_cols: int32 [1024, 16], P('rows', 'probe'), may hold values from 0 to 1023, as said below
Outputs:
- sample: bfloat16 [256, 262144], P('probe', 'rows')
- leaf_factors: float32 [1024, 256, 128], P('rows', 'probe')
- root_factor: float32 [256, 128], P(('rows', 'probe'))
The draws below stay inside these ranges and needn't reach their ends.
Inputs may be any that keep to these rules, and one draw needn't show every extreme that they name: block_cols[c, 0] = c; every other entry of row c lies within 8 of c; away from the first and last 8 clusters it differs from c; entries are reflected at the ends of the fault and may repeat, or equal c, in rows within 8 of either end.
All inputs are finite; a program needn't handle non-finite values.
Results may differ from the reference program's by a relative error of at most 0.00175.
Values may be sent and summed in bfloat16 or wider, within the bound.
A program may use at most 128 MiB of HBM per device.

```python
import jax
import jax.numpy as jnp
from jax import lax

P_SIZE = 256
K = 128
LEAF = 256
NNZ = 16
WIN = 8
CLUSTERS = 1024
N = 262144


def draw_block_cols(key, part):
    key = jax.random.fold_in(key, 7)
    offsets = jnp.concatenate([jnp.arange(-WIN, 0), jnp.arange(1, WIN + 1)]).astype(jnp.int32)
    row_keys = jax.random.split(key, CLUSTERS)
    picked = jax.vmap(lambda row_key: jax.random.permutation(row_key, offsets)[:NNZ - 1])(row_keys)
    steps_away = jnp.concatenate([jnp.zeros((CLUSTERS, 1), jnp.int32), picked], axis=1)
    columns = jnp.arange(CLUSTERS, dtype=jnp.int32)[:, None] + steps_away
    columns = jnp.where(columns < 0, -columns, columns)
    columns = jnp.where(columns > CLUSTERS - 1, 2 * (CLUSTERS - 1) - columns, columns)
    return columns.astype(jnp.int32)


def level_of(rng, dims, cuts, smallest, high):
    loudness = 1.0
    for axis_at, parts in cuts:
        steps = jax.random.uniform(jax.random.fold_in(jax.random.fold_in(rng, 6), axis_at), (parts,), jnp.float32, smallest / len(cuts), high / len(cuts))
        loudness = loudness * jnp.repeat(jnp.exp(steps), dims[axis_at] // parts).reshape((-1,) + (1,) * (len(dims) - 1 - axis_at))
    return loudness


def noise(stream_key, shape, scale, reach, pieces=(), held_as=jnp.bfloat16):
    array = jax.random.normal(stream_key, shape, jnp.float32) * scale
    if len(pieces) > 0:
        array = level_of(stream_key, shape, pieces, -0.22, 0.18) * array
    return jnp.clip(array, min=-reach, max=reach).astype(held_as)


def setup_inputs(seed: int = 0) -> dict:
    key_list = jax.random.split(jax.random.key(seed), 4)
    probe_matrix = noise(key_list[0], (P_SIZE, N), 1.0, 6.0, ((0, 2), (1, 128)))
    near_blocks = noise(key_list[1], (CLUSTERS, NNZ, LEAF, LEAF), (NNZ * LEAF * LEAF // 4) ** -0.5, 0.01171875, ((0, 128), (1, 2)))
    block_cols = draw_block_cols(jax.random.fold_in(key_list[3], 71), 0)
    return {"probe_matrix": probe_matrix, "near_blocks": near_blocks, "block_cols": block_cols}


def compress(stacked):
    head_rows = stacked[:, :K, :]
    gram_cross = jnp.einsum('nkr,npr->nkp', head_rows, stacked, precision=lax.Precision.HIGHEST)
    lower_tri = jnp.linalg.cholesky(gram_cross[:, :, :K])
    factor = jax.scipy.linalg.solve_triangular(lower_tri, gram_cross, lower=True)
    return jnp.swapaxes(factor, 1, 2)

def reference(probe_matrix, near_blocks, block_cols):
    tile_rows = probe_matrix.reshape(P_SIZE, CLUSTERS, LEAF)

    def one_cluster(operands):
        blocks, columns = operands
        picked_tiles = jnp.take(tile_rows, columns, axis=1).astype(jnp.float32)
        return jnp.einsum('nij,pnj->pi', blocks.astype(jnp.float32), picked_tiles)
    sample_full = lax.map(one_cluster, (near_blocks, block_cols))
    sample = jnp.swapaxes(sample_full, 0, 1).reshape(P_SIZE, N).astype(jnp.bfloat16)
    leaf_factors = compress(sample_full)
    factors = leaf_factors
    while factors.shape[0] > 1:
        factors = compress(jnp.concatenate([factors[0::2], factors[1::2]], axis=-1))
    return (sample, leaf_factors, factors[0])
```

```python
import functools

import jax
import jax.numpy as jnp
from jax import lax
from jax.experimental import pallas as pl
from jax.experimental.pallas import tpu as pltpu
from jax.sharding import PartitionSpec as P

K = 128
WIN = 8


def with_halo(block, sides, width):
    for axis, dim in sides:
        count = lax.axis_size(axis)
        forward = [(i, i + 1) for i in range(count - 1)]
        backward = [(target, source) for source, target in forward]
        low = lax.ppermute(
            lax.slice_in_dim(block, block.shape[dim] - width, None, axis=dim), axis, forward
        )
        high = lax.ppermute(lax.slice_in_dim(block, 0, width, axis=dim), axis, backward)
        block = jnp.concatenate([low, block, high], axis=dim)
    return block


def cross_gram(stacked):
    head_rows = stacked[:, :K, :]
    return jnp.einsum("nkr,npr->nkp", head_rows, stacked, precision=lax.Precision.HIGHEST)


def eliminate_panel(groups, first, ncols):
    ng=len(groups)
    iota=lax.broadcasted_iota(jnp.int32,(8,K),0)
    W=groups[0].shape[1]
    nh=W//K
    G=[[g[:,h*K:(h+1)*K] for h in range(nh)] for g in groups]
    for j in range(8*ng):
        c=first+j; gj,sj=divmod(j,8)
        bc=jnp.broadcast_to(G[gj][0][:,c:c+1],(8,K))
        inv=1.0/bc[sj:sj+1,:]
        rows=[G[gj][h][sj:sj+1,:]*inv for h in range(nh)]
        for g in range(gj,ng):
            if g==gj:
                if sj==7: continue
                m=jnp.where(iota>sj,bc,0.0)
            else:
                m=jnp.broadcast_to(G[g][0][:,c:c+1],(8,K))
            for h in range(nh):
                G[g][h]=G[g][h]-m*rows[h]
    return G
def factor_many(a_ref, ms, b, W=2*K):
    ng=b//8
    lane=lax.broadcasted_iota(jnp.int32,(8,K),1)
    sub=lax.broadcasted_iota(jnp.int32,(8,K),0)
    for k in range(K//b):
        outs=[]
        for m in ms:
            P=[a_ref[m,k*b+8*g:k*b+8*g+8,:] for g in range(ng)]
            outs.append(P)
        res=[eliminate_panel(P,k*b,b) for P in outs]
        for m,G in zip(ms,res):
            full=[]
            for g in range(ng):
                r0=k*b+8*g
                d=jnp.sum(jnp.where(lane==r0+sub,G[g][0],0.0),axis=1,keepdims=True)
                rs=lax.rsqrt(d)
                G[g][0]=jnp.where(lane>=r0+sub,G[g][0]*rs,0.0)
                for h in range(1,len(G[g])): G[g][h]=G[g][h]*rs
                row=jnp.concatenate(G[g],axis=1)
                a_ref[m,r0:r0+8,:]=row
                full.append(row)
            if (k+1)*b<K:
                R=jnp.concatenate(full,axis=0)
                left=R[:,:K].T[(k+1)*b:,:]
                a_ref[m,(k+1)*b:,:]=a_ref[m,(k+1)*b:,:]-jnp.dot(left,R,precision=lax.Precision.HIGHEST,preferred_element_type=jnp.float32)
def kernel(c_ref,o_ref,a_ref,*,b,groups):
    a_ref[...]=c_ref[...]
    for ms in groups:
        factor_many(a_ref,ms,b)
    for m in range(c_ref.shape[0]):
        o_ref[m]=a_ref[m].T
def call(c,b,groups):
    nb=c.shape[0]
    return pl.pallas_call(functools.partial(kernel,b=b,groups=groups),
      out_shape=jax.ShapeDtypeStruct((nb,2*K,K),jnp.float32),
      in_specs=[pl.BlockSpec(memory_space=pltpu.VMEM)],out_specs=pl.BlockSpec(memory_space=pltpu.VMEM),
      scratch_shapes=[pltpu.VMEM((nb,K,2*K),jnp.float32)],
      name="factor")(c)
def local(probe_matrix, near_blocks, block_cols):
    clusters_dev = near_blocks.shape[0]
    leaf_rows = near_blocks.shape[2]
    columns_dev = probe_matrix.shape[0]
    extended = with_halo(probe_matrix, (("rows", 1),), WIN * leaf_rows)
    local_cols = block_cols - (lax.axis_index("rows") * clusters_dev - WIN)
    rows_piece = lax.all_gather(extended, "probe", axis=0, tiled=True)
    tile_rows = rows_piece.reshape(rows_piece.shape[0], -1, leaf_rows)
    picked_tiles = jnp.take(tile_rows, local_cols, axis=1)
    partial_sample = jnp.einsum(
        "cnij,pcnj->cpi", near_blocks, picked_tiles, preferred_element_type=jnp.float32
    )
    own_part = lax.psum_scatter(partial_sample, "probe", scatter_dimension=1, tiled=True)
    full_sample = lax.all_gather(own_part, "probe", axis=1, tiled=True)
    sample = (
        jnp.swapaxes(own_part, 0, 1)
        .reshape(columns_dev, clusters_dev * leaf_rows)
        .astype(jnp.bfloat16)
    )
    leaf_grams = cross_gram(full_sample)
    root_gram = lax.psum(jnp.sum(leaf_grams, axis=0), "rows")
    factors = call(jnp.concatenate([leaf_grams, root_gram[None]], axis=0), 16, [list(range(clusters_dev + 1))])
    leaf_out = lax.dynamic_slice_in_dim(
        factors[:clusters_dev], lax.axis_index("probe") * columns_dev, columns_dev, 1
    )
    root = factors[clusters_dev]
    share_rows = root.shape[0] // (lax.axis_size("rows") * lax.axis_size("probe"))
    device_slot = lax.axis_index("rows") * lax.axis_size("probe") + lax.axis_index("probe")
    root_out = lax.dynamic_slice_in_dim(root, device_slot * share_rows, share_rows, 0)
    return (sample, leaf_out, root_out)


def solution(mesh):
    placed = (P("probe", "rows"), P("rows", "probe", None, None), P("rows", "probe"))
    return jax.shard_map(
        local,
        mesh=mesh,
        in_specs=placed,
        out_specs=(P("probe", "rows"), P("rows", "probe", None), P(("rows", "probe"), None)),
        check_vma=False,
    )
```

```python
import functools

import jax
import jax.numpy as jnp
from jax import lax
from jax.experimental import pallas as pl
from jax.experimental.pallas import tpu as pltpu
from jax.sharding import PartitionSpec as P

K = 128
LEAF = 256
PLANE = 16
HIGH = lax.Precision.HIGHEST
ORDER = (3, 4, 2, 5, 1, 6, 0, 7)


def cross(a, b, precision=None):
    return lax.dot_general(
        a, b, (((1,), (1,)), ((), ())), precision=precision, preferred_element_type=jnp.float32
    )


def gather_kernel(
    depth, cols_ref, probe_ref, blocks_ref,
    sample_ref, grams_ref, root_ref,
    own, landing, window, blocks, mine, theirs, total, rs_buf, z_buf,
    block_sem, own_sem, share_send, share_recv, halo_send, halo_recv, pass_send, pass_recv,
    part_send, part_recv, rs_send, rs_recv, z_send, z_recv, ag_send, ag_recv,
):
    row, core = lax.axis_index("rows"), lax.axis_index("probe")
    rows = PLANE * depth
    sibling = (row, 1 - core)
    after, before = (lax.rem(row + 1, rows), core), (lax.rem(row + rows - 1, rows), core)
    layer, spot = row // PLANE, lax.rem(row, PLANE)

    def in_plane(step):
        return (layer * PLANE + lax.rem(spot + step, PLANE), core)

    def in_column(step):
        return (lax.rem(layer + step, depth) * PLANE + spot, core)

    barrier = pltpu.get_barrier_semaphore()
    for target in (after, before, sibling):
        pl.semaphore_signal(barrier, inc=1, device_id=target, device_id_type=pl.DeviceIdType.MESH)

    def greet_plane(step, carry):
        pl.semaphore_signal(barrier, inc=1, device_id=in_plane(step), device_id_type=pl.DeviceIdType.MESH)
        return carry

    def greet_column(step, carry):
        pl.semaphore_signal(barrier, inc=1, device_id=in_column(step), device_id_type=pl.DeviceIdType.MESH)
        return carry

    lax.fori_loop(1, PLANE, greet_plane, 0)
    lax.fori_loop(1, depth, greet_column, 0)

    own_copy = pltpu.make_async_copy(probe_ref, own.at[core], own_sem)
    own_copy.start()
    block_copies = {}
    for c in ORDER:
        block_copies[c] = pltpu.make_async_copy(blocks_ref.at[c], blocks.at[c], block_sem.at[c])
        block_copies[c].start()
    pl.semaphore_wait(barrier, 3 + PLANE - 1 + depth - 1)

    def remote(src, dst, send, recv, target):
        return pltpu.make_async_remote_copy(
            src_ref=src, dst_ref=dst, send_sem=send, recv_sem=recv,
            device_id=target, device_id_type=pl.DeviceIdType.MESH,
        )

    halo = {}
    for t in range(8):
        for side, c, target in ((0, 7 - t, after), (1, t, before)):
            halo[side, t] = remote(
                probe_ref.at[:, c * LEAF:(c + 1) * LEAF], landing.at[side, c, core],
                halo_send.at[side, c], halo_recv.at[side, c], target,
            )
            halo[side, t].start()
    share = remote(probe_ref, own.at[core], share_send, share_recv, sibling)
    share.start()

    own_copy.wait()
    share.wait_recv()
    for c in range(8):
        for half in range(2):
            window[8 + c, half * K:(half + 1) * K, :] = own[half, :, c * LEAF:(c + 1) * LEAF]

    passed = {}
    parts = {}

    def absorb(t):
        for side, c in ((0, 7 - t), (1, t)):
            passed[side, t].wait_recv()
            for half in range(2):
                window[16 * side + c, half * K:(half + 1) * K, :] = landing[side, c, half]

    def multiply(c):
        block_copies[c].wait()
        acc = jnp.zeros((LEAF, LEAF), jnp.float32)
        for b in range(8):
            at = jnp.clip(cols_ref[c, b] - (row * 8 - 8), 0, 23)
            acc = acc + cross(window[at], blocks[c, b])
        mine[c] = acc
        parts[c] = remote(mine.at[c], theirs.at[c], part_send.at[c], part_recv.at[c], sibling)
        parts[c].start()

    def gram(c, first):
        parts[c].wait_recv()
        full = mine[c] + theirs[c]
        theirs[c] = full
        kept = theirs[c, pl.ds(pl.multiple_of(core * K, K), K), :]
        sample_ref[:, c * LEAF:(c + 1) * LEAF] = kept.astype(jnp.bfloat16)
        g = cross(full[:K], full, HIGH)
        grams_ref[c] = g
        total[...] = g if first else total[...] + g

    for t in range(8):
        for side, c in ((0, 7 - t), (1, t)):
            halo[side, t].wait_recv()
            passed[side, t] = remote(
                landing.at[side, c, core], landing.at[side, c, core],
                pass_send.at[side, c], pass_recv.at[side, c], sibling,
            )
            passed[side, t].start()
        absorb(t)
        if t >= 4:
            for c in (7 - t, t):
                multiply(c)
        if t >= 5:
            for c in (8 - t, t - 1):
                gram(c, c == 3)
    for c in (0, 7):
        gram(c, False)

    def scatter(step, carry):
        at = pl.multiple_of(lax.rem(spot + step, PLANE) * 8, 8)
        remote(total.at[pl.ds(at, 8), :], rs_buf.at[step], rs_send.at[step], rs_recv.at[step], in_plane(step)).start()
        return carry

    def scattered(step, carry):
        remote(total.at[pl.ds(0, 8), :], rs_buf.at[step], rs_send.at[step], rs_recv.at[step], in_plane(step)).wait()
        return carry

    lax.fori_loop(1, PLANE, scatter, 0)
    rs_buf[0] = total[pl.ds(pl.multiple_of(spot * 8, 8), 8), :]
    lax.fori_loop(1, PLANE, scattered, 0)
    z_buf[0] = jnp.sum(rs_buf[...], axis=0)

    def column(step):
        return remote(z_buf.at[0], z_buf.at[step], z_send.at[step], z_recv.at[step], in_column(step))

    def spread(step, carry):
        column(step).start()
        return carry

    def gathered(step, carry):
        column(step).wait()
        return carry

    lax.fori_loop(1, depth, spread, 0)
    lax.fori_loop(1, depth, gathered, 0)
    here = pl.ds(pl.multiple_of(spot * 8, 8), 8)
    root_ref[here, :] = jnp.sum(z_buf[...], axis=0)

    def publish(step):
        return remote(root_ref.at[here, :], root_ref.at[here, :], ag_send.at[step], ag_recv.at[step], in_plane(step))

    def published(step, carry):
        publish(step).start()
        return carry

    def finished(step, carry):
        publish(step).wait_send()
        from_row = pl.ds(pl.multiple_of(lax.rem(spot + PLANE - step, PLANE) * 8, 8), 8)
        remote(root_ref.at[from_row, :], root_ref.at[from_row, :], ag_send.at[step], ag_recv.at[step], in_plane(step)).wait_recv()
        return carry

    lax.fori_loop(1, PLANE, published, 0)
    lax.fori_loop(1, PLANE, finished, 0)

    share.wait_send()
    for copy in list(halo.values()) + list(passed.values()) + list(parts.values()):
        copy.wait_send()


def gather(block_cols, probe_matrix, near_blocks):
    depth = lax.axis_size("rows") // PLANE
    bf16, f32, dma = jnp.bfloat16, jnp.float32, pltpu.SemaphoreType.DMA
    whole = pl.BlockSpec(memory_space=pltpu.VMEM)
    return pl.pallas_call(
        functools.partial(gather_kernel, depth),
        out_shape=(
            jax.ShapeDtypeStruct((K, 8 * LEAF), bf16),
            jax.ShapeDtypeStruct((8, K, LEAF), f32),
            jax.ShapeDtypeStruct((K, LEAF), f32),
        ),
        in_specs=[
            pl.BlockSpec(memory_space=pltpu.SMEM),
            pl.BlockSpec(memory_space=pl.ANY),
            pl.BlockSpec(memory_space=pl.ANY),
        ],
        out_specs=(whole, whole, whole),
        scratch_shapes=[
            pltpu.VMEM((2, K, 8 * LEAF), bf16),
            pltpu.VMEM((2, 8, 2, K, LEAF), bf16),
            pltpu.VMEM((24, LEAF, LEAF), bf16),
            pltpu.VMEM((8, 8, LEAF, LEAF), bf16),
            pltpu.VMEM((8, LEAF, LEAF), f32),
            pltpu.VMEM((8, LEAF, LEAF), f32),
            pltpu.VMEM((K, LEAF), f32),
            pltpu.VMEM((PLANE, 8, LEAF), f32),
            pltpu.VMEM((depth, 8, LEAF), f32),
            dma((8,)), dma, dma, dma, dma((2, 8)), dma((2, 8)), dma((2, 8)), dma((2, 8)),
            dma((8,)), dma((8,)), dma((PLANE,)), dma((PLANE,)),
            dma((depth,)), dma((depth,)), dma((PLANE,)), dma((PLANE,)),
        ],
        compiler_params=pltpu.CompilerParams(
            collective_id=0, has_side_effects=True, vmem_limit_bytes=40 * 2**20
        ),
        name="gather",
    )(block_cols, probe_matrix, near_blocks)


def eliminate_panel(groups, first, ncols):
    ng=len(groups)
    iota=lax.broadcasted_iota(jnp.int32,(8,K),0)
    W=groups[0].shape[1]
    nh=W//K
    G=[[g[:,h*K:(h+1)*K] for h in range(nh)] for g in groups]
    for j in range(8*ng):
        c=first+j; gj,sj=divmod(j,8)
        bc=jnp.broadcast_to(G[gj][0][:,c:c+1],(8,K))
        inv=1.0/bc[sj:sj+1,:]
        rows=[G[gj][h][sj:sj+1,:]*inv for h in range(nh)]
        for g in range(gj,ng):
            if g==gj:
                if sj==7: continue
                m=jnp.where(iota>sj,bc,0.0)
            else:
                m=jnp.broadcast_to(G[g][0][:,c:c+1],(8,K))
            for h in range(nh):
                G[g][h]=G[g][h]-m*rows[h]
    return G
def factor_many(a_ref, ms, b, W=2*K):
    ng=b//8
    lane=lax.broadcasted_iota(jnp.int32,(8,K),1)
    sub=lax.broadcasted_iota(jnp.int32,(8,K),0)
    for k in range(K//b):
        outs=[]
        for m in ms:
            P=[a_ref[m,k*b+8*g:k*b+8*g+8,:] for g in range(ng)]
            outs.append(P)
        res=[eliminate_panel(P,k*b,b) for P in outs]
        for m,G in zip(ms,res):
            full=[]
            for g in range(ng):
                r0=k*b+8*g
                d=jnp.sum(jnp.where(lane==r0+sub,G[g][0],0.0),axis=1,keepdims=True)
                rs=lax.rsqrt(d)
                G[g][0]=jnp.where(lane>=r0+sub,G[g][0]*rs,0.0)
                for h in range(1,len(G[g])): G[g][h]=G[g][h]*rs
                row=jnp.concatenate(G[g],axis=1)
                a_ref[m,r0:r0+8,:]=row
                full.append(row)
            if (k+1)*b<K:
                R=jnp.concatenate(full,axis=0)
                left=R[:,:K].T[(k+1)*b:,:]
                a_ref[m,(k+1)*b:,:]=a_ref[m,(k+1)*b:,:]-jnp.dot(left,R,precision=lax.Precision.HIGHEST,preferred_element_type=jnp.float32)


def factor_kernel(grams_ref, c_ref, leaf_ref, out_ref, a_ref, f_ref):
    count = grams_ref.shape[0]
    a_ref[0:count] = grams_ref[...]
    a_ref[count] = c_ref[...]
    factor_many(a_ref, list(range(count + 1)), 16)
    core = lax.axis_index("probe")
    half = pl.ds(pl.multiple_of(core * K, K), K)
    for m in range(count):
        leaf_ref[m] = a_ref[m, :, half].T
    f_ref[...] = a_ref[count].T
    out_ref[...] = f_ref[pl.ds(lax.axis_index("rows") * 2 + core, 1), :]


def factor(grams, root_gram):
    count = grams.shape[0]
    whole = pl.BlockSpec(memory_space=pltpu.VMEM)
    return pl.pallas_call(
        factor_kernel,
        out_shape=(
            jax.ShapeDtypeStruct((count, K, K), jnp.float32),
            jax.ShapeDtypeStruct((1, K), jnp.float32),
        ),
        in_specs=[whole, whole],
        out_specs=(whole, whole),
        scratch_shapes=[
            pltpu.VMEM((count + 1, K, 2 * K), jnp.float32),
            pltpu.VMEM((2 * K, K), jnp.float32),
        ],
        name="factor",
    )(grams, root_gram)


def local(probe_matrix, near_blocks, block_cols):
    sample, grams, root_gram = gather(block_cols, probe_matrix, near_blocks)
    leaf_out, root_out = factor(grams, root_gram)
    return (sample, leaf_out, root_out)


def solution(mesh):
    placed = (P("probe", "rows"), P("rows", "probe", None, None), P("rows", "probe"))
    return jax.shard_map(
        local,
        mesh=mesh,
        in_specs=placed,
        out_specs=(P("probe", "rows"), P("rows", "probe", None), P(("rows", "probe"), None)),
        check_vma=False,
    )
```

```python
import functools

import jax
import jax.numpy as jnp
from jax import lax
from jax.experimental import pallas as pl
from jax.experimental.pallas import tpu as pltpu
from jax.sharding import PartitionSpec as P

K = 128
LEAF = 256
PLANE = 16
PANEL = 16
HIGH = lax.Precision.HIGHEST
ORDER = (3, 4, 2, 5, 1, 6, 0, 7)


def cross(a, b, precision=None):
    return lax.dot_general(
        a, b, (((1,), (1,)), ((), ())), precision=precision, preferred_element_type=jnp.float32
    )


def gather_kernel(
    depth, cols_ref, probe_ref, blocks_ref,
    sample_ref, grams_ref, root_ref,
    own, landing, window, blocks, mine, theirs, total, rs_buf, z_buf,
    meet, block_sem, own_sem, share_send, share_recv, halo_send, halo_recv, pass_send, pass_recv,
    part_send, part_recv, rs_send, rs_recv, z_send, z_recv, ag_send, ag_recv,
):
    row, core = lax.axis_index("rows"), lax.axis_index("probe")
    rows = PLANE * depth
    sibling = (row, 1 - core)
    after, before = (lax.rem(row + 1, rows), core), (lax.rem(row + rows - 1, rows), core)
    layer, spot = row // PLANE, lax.rem(row, PLANE)

    side, front = lax.rem(spot, 4), spot // 4

    def in_plane(step):
        return (layer * PLANE + lax.rem(spot + step, PLANE), core)

    def in_column(step):
        return (lax.rem(layer + step, depth) * PLANE + spot, core)

    along_x = [(layer * PLANE + front * 4 + lax.rem(side + d, 4), core) for d in (1, 3)]
    along_y = [in_plane(4), in_plane(12)]
    along_z = [in_column(1), in_column(depth - 1)]

    def greet(semaphore, targets):
        for target in targets:
            pl.semaphore_signal(semaphore, inc=1, device_id=target, device_id_type=pl.DeviceIdType.MESH)

    own_copies = {}
    for c in (7, 0, 6, 1, 5, 2, 4, 3):
        own_copies[c] = pltpu.make_async_copy(
            probe_ref.at[:, c * LEAF:(c + 1) * LEAF], own.at[core, c], own_sem.at[c]
        )
        own_copies[c].start()
    barrier = pltpu.get_barrier_semaphore()
    entered = [after, before, sibling] + along_x + along_y + along_z
    greet(barrier, entered)
    pl.semaphore_wait(barrier, len(entered))

    def remote(src, dst, send, recv, target):
        return pltpu.make_async_remote_copy(
            src_ref=src, dst_ref=dst, send_sem=send, recv_sem=recv,
            device_id=target, device_id_type=pl.DeviceIdType.MESH,
        )

    rounds = [(meet.at[0], along_x, meet.at[1], along_z), (meet.at[2], along_y, meet.at[3], along_z),
              (meet.at[4], along_y, meet.at[5], along_z)]

    def announce(n):
        greet(rounds[n][0], rounds[n][1])
        greet(rounds[n][2], rounds[n][3])

    def learn(n):
        pl.semaphore_wait(rounds[n][0], 2)
        pl.semaphore_wait(rounds[n][2], 2)

    halo = {}
    waited = set()
    for t in range(8):
        for side_of, c, target in ((0, 7 - t, after), (1, t, before)):
            if c not in waited:
                own_copies[c].wait()
                waited.add(c)
            halo[side_of, t] = remote(
                own.at[core, c], landing.at[side_of, c, core],
                halo_send.at[side_of, c], halo_recv.at[side_of, c], target,
            )
            halo[side_of, t].start()
    share = remote(own.at[core], own.at[core], share_send, share_recv, sibling)
    share.start()
    announce(0)
    block_copies = {}
    for c in ORDER:
        block_copies[c] = pltpu.make_async_copy(blocks_ref.at[c], blocks.at[c], block_sem.at[c])
        block_copies[c].start()
    share.wait_recv()
    for c in range(8):
        for half in range(2):
            window[8 + c, half * K:(half + 1) * K, :] = own[half, c]

    passed = {}
    parts = {}

    def absorb(t):
        for side, c in ((0, 7 - t), (1, t)):
            passed[side, t].wait_recv()
            for half in range(2):
                window[16 * side + c, half * K:(half + 1) * K, :] = landing[side, c, half]

    def multiply(c):
        block_copies[c].wait()
        acc = jnp.zeros((LEAF, LEAF), jnp.float32)
        for b in range(8):
            at = jnp.clip(cols_ref[c, b] - (row * 8 - 8), 0, 23)
            acc = acc + cross(window[at], blocks[c, b])
        mine[c] = acc
        parts[c] = remote(mine.at[c], theirs.at[c], part_send.at[c], part_recv.at[c], sibling)
        parts[c].start()

    def gram(c, first):
        parts[c].wait_recv()
        full = mine[c] + theirs[c]
        theirs[c] = full
        kept = theirs[c, pl.ds(pl.multiple_of(core * K, K), K), :]
        sample_ref[:, c * LEAF:(c + 1) * LEAF] = kept.astype(jnp.bfloat16)
        g = cross(full[:K], full, HIGH)
        grams_ref[c] = g
        total[...] = g if first else total[...] + g

    for t in range(8):
        for side, c in ((0, 7 - t), (1, t)):
            halo[side, t].wait_recv()
            passed[side, t] = remote(
                landing.at[side, c, core], landing.at[side, c, core],
                pass_send.at[side, c], pass_recv.at[side, c], sibling,
            )
            passed[side, t].start()
        absorb(t)
        if 1 <= t <= 3:
            learn(t - 1)
            if t < 3:
                announce(t)
        if t >= 4:
            for c in (7 - t, t):
                multiply(c)
        if t >= 5:
            for c in (8 - t, t - 1):
                gram(c, c == 3)
    for c in (0, 7):
        gram(c, False)

    def scatter(step, carry):
        at = pl.multiple_of(lax.rem(spot + step, PLANE) * 8, 8)
        remote(total.at[pl.ds(at, 8), :], rs_buf.at[step], rs_send.at[step], rs_recv.at[step], in_plane(step)).start()
        return carry

    def scattered(step, carry):
        remote(total.at[pl.ds(0, 8), :], rs_buf.at[step], rs_send.at[step], rs_recv.at[step], in_plane(step)).wait()
        return carry

    lax.fori_loop(1, PLANE, scatter, 0)
    rs_buf[0] = total[pl.ds(pl.multiple_of(spot * 8, 8), 8), :]
    lax.fori_loop(1, PLANE, scattered, 0)
    z_buf[0] = jnp.sum(rs_buf[...], axis=0)

    def column(step):
        return remote(z_buf.at[0], z_buf.at[step], z_send.at[step], z_recv.at[step], in_column(step))

    def spread(step, carry):
        column(step).start()
        return carry

    def gathered(step, carry):
        column(step).wait()
        return carry

    lax.fori_loop(1, depth, spread, 0)
    lax.fori_loop(1, depth, gathered, 0)
    here = pl.ds(pl.multiple_of(spot * 8, 8), 8)
    root_ref[here, :] = jnp.sum(z_buf[...], axis=0)

    def publish(step):
        return remote(root_ref.at[here, :], root_ref.at[here, :], ag_send.at[step], ag_recv.at[step], in_plane(step))

    def published(step, carry):
        publish(step).start()
        return carry

    def finished(step, carry):
        publish(step).wait_send()
        from_row = pl.ds(pl.multiple_of(lax.rem(spot + PLANE - step, PLANE) * 8, 8), 8)
        remote(root_ref.at[from_row, :], root_ref.at[from_row, :], ag_send.at[step], ag_recv.at[step], in_plane(step)).wait_recv()
        return carry

    lax.fori_loop(1, PLANE, published, 0)
    lax.fori_loop(1, PLANE, finished, 0)

    share.wait_send()
    for copy in list(halo.values()) + list(passed.values()) + list(parts.values()):
        copy.wait_send()


def gather(block_cols, probe_matrix, near_blocks):
    depth = lax.axis_size("rows") // PLANE
    bf16, f32, dma = jnp.bfloat16, jnp.float32, pltpu.SemaphoreType.DMA
    whole = pl.BlockSpec(memory_space=pltpu.VMEM)
    return pl.pallas_call(
        functools.partial(gather_kernel, depth),
        out_shape=(
            jax.ShapeDtypeStruct((K, 8 * LEAF), bf16),
            jax.ShapeDtypeStruct((8, K, LEAF), f32),
            jax.ShapeDtypeStruct((K, LEAF), f32),
        ),
        in_specs=[
            pl.BlockSpec(memory_space=pltpu.SMEM),
            pl.BlockSpec(memory_space=pltpu.HBM),
            pl.BlockSpec(memory_space=pltpu.HBM),
        ],
        out_specs=(whole, whole, whole),
        scratch_shapes=[
            pltpu.VMEM((2, 8, K, LEAF), bf16),
            pltpu.VMEM((2, 8, 2, K, LEAF), bf16),
            pltpu.VMEM((24, LEAF, LEAF), bf16),
            pltpu.VMEM((8, 8, LEAF, LEAF), bf16),
            pltpu.VMEM((8, LEAF, LEAF), f32),
            pltpu.VMEM((8, LEAF, LEAF), f32),
            pltpu.VMEM((K, LEAF), f32),
            pltpu.VMEM((PLANE, 8, LEAF), f32),
            pltpu.VMEM((depth, 8, LEAF), f32),
            pltpu.SemaphoreType.REGULAR((6,)), dma((8,)), dma((8,)), dma, dma, dma((2, 8)), dma((2, 8)), dma((2, 8)), dma((2, 8)),
            dma((8,)), dma((8,)), dma((PLANE,)), dma((PLANE,)),
            dma((depth,)), dma((depth,)), dma((PLANE,)), dma((PLANE,)),
        ],
        compiler_params=pltpu.CompilerParams(
            collective_id=0, has_side_effects=True, vmem_limit_bytes=56 * 2**20
        ),
        name="gather",
    )(block_cols, probe_matrix, near_blocks)


SUB = 8


def eliminate_block(rows, c0, bs):
    e={}
    for j in range(bs):
        for i in range(j,bs):
            e[j,i]=jnp.broadcast_to(rows[j][0][:,c0+i:c0+i+1],(SUB,K))
    for j in range(bs):
        rs=lax.rsqrt(e[j,j])
        f={i:e[j,i]*rs for i in range(j+1,bs)}
        rows[j]=[h*rs for h in rows[j]]
        for i in range(j+1,bs):
            for i2 in range(i,bs):
                e[i,i2]=e[i,i2]-f[i]*f[i2]
            rows[i]=[h-f[i]*p for h,p in zip(rows[i],rows[j])]
    for i in range(bs,len(rows)):
        for j in range(bs):
            f=jnp.broadcast_to(rows[j][0][:,c0+i:c0+i+1],(SUB,K))
            rows[i]=[h-f*p for h,p in zip(rows[i],rows[j])]
    return rows
def factor_groups(a_refs, t_refs, b, bs):
    lane=lax.broadcasted_iota(jnp.int32,(b,K),1)
    sub=lax.broadcasted_iota(jnp.int32,(b,K),0)
    for k in range(K//b):
        r0=k*b
        panels=[]
        for (a_ref,m),(t0,t1) in zip(a_refs,t_refs):
            rows=[]
            if m==1:
                for r in range(b):
                    rows.append([jnp.broadcast_to(a_ref[0,r0+r:r0+r+1,h*K:(h+1)*K],(SUB,K)) for h in range(2)])
            else:
                for s in range(m):
                    t0[pl.ds(s,b,stride=SUB),:]=a_ref[s,r0:r0+b,0:K]
                    t1[pl.ds(s,b,stride=SUB),:]=a_ref[s,r0:r0+b,K:2*K]
                for r in range(b):
                    rows.append([t[SUB*r:SUB*r+SUB,:] for t in (t0,t1)])
            panels.append(rows)
        for c in range(0,b,bs):
            for g in range(len(panels)):
                rest=eliminate_block(panels[g][c:],r0+c,bs)
                panels[g]=panels[g][:c]+rest
        for (a_ref,m),(t0,t1),rows in zip(a_refs,t_refs,panels):
            for r in range(b):
                t0[SUB*r:SUB*r+SUB,:]=rows[r][0]
                t1[SUB*r:SUB*r+SUB,:]=rows[r][1]
            for s in range(m):
                low=t0[pl.ds(s,b,stride=SUB),:]
                high=t1[pl.ds(s,b,stride=SUB),:]
                low=jnp.where(lane>=r0+sub,low,0.0)
                a_ref[s,r0:r0+b,0:K]=low
                a_ref[s,r0:r0+b,K:2*K]=high
                if r0+b<K:
                    left=low.T[r0+b:,:]
                    right=jnp.concatenate([low,high],axis=1)
                    a_ref[s,r0+b:,:]=a_ref[s,r0+b:,:]-jnp.dot(left,right,precision=lax.Precision.HIGHEST,preferred_element_type=jnp.float32)


def factor_kernel(grams_ref, c_ref, leaf_ref, out_ref, a_ref, r_ref, f_ref, t0, t1, t2, t3):
    count = grams_ref.shape[0]
    a_ref[...] = grams_ref[...]
    r_ref[0] = c_ref[...]
    factor_groups([(a_ref, count), (r_ref, 1)], [(t0, t1), (t2, t3)], PANEL, 8)
    core = lax.axis_index("probe")
    half = pl.ds(pl.multiple_of(core * K, K), K)
    for m in range(count):
        leaf_ref[m] = a_ref[m, :, half].T
    f_ref[...] = r_ref[0].T
    out_ref[...] = f_ref[pl.ds(lax.axis_index("rows") * 2 + core, 1), :]


def factor(grams, root_gram):
    count = grams.shape[0]
    whole = pl.BlockSpec(memory_space=pltpu.VMEM)
    rows = pltpu.VMEM((PANEL * SUB, K), jnp.float32)
    return pl.pallas_call(
        factor_kernel,
        out_shape=(
            jax.ShapeDtypeStruct((count, K, K), jnp.float32),
            jax.ShapeDtypeStruct((1, K), jnp.float32),
        ),
        in_specs=[whole, whole],
        out_specs=(whole, whole),
        scratch_shapes=[
            pltpu.VMEM((count, K, 2 * K), jnp.float32),
            pltpu.VMEM((1, K, 2 * K), jnp.float32),
            pltpu.VMEM((2 * K, K), jnp.float32),
            rows, rows, rows, rows,
        ],
        name="factor",
    )(grams, root_gram)


def local(probe_matrix, near_blocks, block_cols):
    sample, grams, root_gram = gather(block_cols, probe_matrix, near_blocks)
    leaf_out, root_out = factor(grams, root_gram)
    return (sample, leaf_out, root_out)


def solution(mesh):
    placed = (P("probe", "rows"), P("rows", "probe", None, None), P("rows", "probe"))
    return jax.shard_map(
        local,
        mesh=mesh,
        in_specs=placed,
        out_specs=(P("probe", "rows"), P("rows", "probe", None), P(("rows", "probe"), None)),
        check_vma=False,
    )
```

```python
import functools

import jax
import jax.numpy as jnp
from jax import lax
from jax.experimental import pallas as pl
from jax.experimental.pallas import tpu as pltpu
from jax.sharding import PartitionSpec as P

K = 128
LEAF = 256
PLANE = 16
PANEL = 16
BLOCK = 8
SUB = 8
HIGH = lax.Precision.HIGHEST
MESH = pl.DeviceIdType.MESH


def cross(a, b, precision=None):
    return lax.dot_general(
        a, b, (((1,), (1,)), ((), ())), precision=precision, preferred_element_type=jnp.float32
    )


def eliminate_block(rows, c0):
    e = {}
    for j in range(BLOCK):
        for i in range(j, BLOCK):
            e[j, i] = jnp.broadcast_to(rows[j][0][:, c0 + i:c0 + i + 1], (SUB, K))
    for j in range(BLOCK):
        rs = lax.rsqrt(e[j, j])
        f = {i: e[j, i] * rs for i in range(j + 1, BLOCK)}
        rows[j] = [h * rs for h in rows[j]]
        for i in range(j + 1, BLOCK):
            for i2 in range(i, BLOCK):
                e[i, i2] = e[i, i2] - f[i] * f[i2]
            rows[i] = [h - f[i] * p for h, p in zip(rows[i], rows[j])]
    for i in range(BLOCK, len(rows)):
        for j in range(BLOCK):
            f = jnp.broadcast_to(rows[j][0][:, c0 + i:c0 + i + 1], (SUB, K))
            rows[i] = [h - f * p for h, p in zip(rows[i], rows[j])]
    return rows


def factor_panel(a_ref, count, t0, t1, k):
    r0 = k * PANEL
    lane = lax.broadcasted_iota(jnp.int32, (PANEL, K), 1)
    sub = lax.broadcasted_iota(jnp.int32, (PANEL, K), 0)
    if count == 1:
        rows = [
            [jnp.broadcast_to(a_ref[0, r0 + r:r0 + r + 1, h * K:(h + 1) * K], (SUB, K)) for h in range(2)]
            for r in range(PANEL)
        ]
    else:
        for s in range(count):
            t0[pl.ds(s, PANEL, stride=SUB), :] = a_ref[s, r0:r0 + PANEL, 0:K]
            t1[pl.ds(s, PANEL, stride=SUB), :] = a_ref[s, r0:r0 + PANEL, K:2 * K]
        rows = [[t[SUB * r:SUB * r + SUB, :] for t in (t0, t1)] for r in range(PANEL)]
    for c in range(0, PANEL, BLOCK):
        rows = rows[:c] + eliminate_block(rows[c:], r0 + c)
    for r in range(PANEL):
        t0[SUB * r:SUB * r + SUB, :] = rows[r][0]
        t1[SUB * r:SUB * r + SUB, :] = rows[r][1]
    for s in range(count):
        low = jnp.where(lane >= r0 + sub, t0[pl.ds(s, PANEL, stride=SUB), :], 0.0)
        high = t1[pl.ds(s, PANEL, stride=SUB), :]
        a_ref[s, r0:r0 + PANEL, 0:K] = low
        a_ref[s, r0:r0 + PANEL, K:2 * K] = high
        if r0 + PANEL < K:
            left = low.T[r0 + PANEL:, :]
            right = jnp.concatenate([low, high], axis=1)
            a_ref[s, r0 + PANEL:, :] = a_ref[s, r0 + PANEL:, :] - jnp.dot(
                left, right, precision=HIGH, preferred_element_type=jnp.float32
            )


def gather_kernel(
    depth, cols_ref, probe_ref, blocks_ref,
    sample_ref, leaf_ref, root_ref,
    own, landing, window, blocks, given, kept, theirs, stage, sent_stage, total, rs_buf, z_buf,
    leaf_a, t0, t1, leaf_buf, sent_leaf,
    meet, block_sem, own_sem, share_send, share_recv, halo_send, halo_recv, pass_send, pass_recv,
    part_send, part_recv, tile_send, tile_recv, out_sem, leaf_send, leaf_recv, leaf_sem,
    rs_send, rs_recv, z_send, z_recv, ag_send, ag_recv,
):
    row, core = lax.axis_index("rows"), lax.axis_index("probe")
    rows = PLANE * depth
    sibling = (row, 1 - core)
    after, before = (lax.rem(row + 1, rows), core), (lax.rem(row + rows - 1, rows), core)
    layer, spot = row // PLANE, lax.rem(row, PLANE)
    side, front = lax.rem(spot, 4), spot // 4

    def in_plane(step):
        return (layer * PLANE + lax.rem(spot + step, PLANE), core)

    def in_column(step):
        return (lax.rem(layer + step, depth) * PLANE + spot, lax.rem(core + step // depth, 2))

    along_x = [(layer * PLANE + front * 4 + lax.rem(side + d, 4), core) for d in (1, 3)]
    along_y = [in_plane(4), in_plane(12)]
    along_z = [in_column(1), in_column(depth - 1)]

    def greet(semaphore, targets):
        for target in targets:
            pl.semaphore_signal(semaphore, inc=1, device_id=target, device_id_type=MESH)

    def remote(src, dst, send, recv, target):
        return pltpu.make_async_remote_copy(
            src_ref=src, dst_ref=dst, send_sem=send, recv_sem=recv,
            device_id=target, device_id_type=MESH,
        )

    own_copies = {}
    for c in (7, 0, 6, 1, 5, 2, 4, 3):
        own_copies[c] = pltpu.make_async_copy(
            probe_ref.at[:, c * LEAF:(c + 1) * LEAF], own.at[core, c], own_sem.at[c]
        )
        own_copies[c].start()
    barrier = pltpu.get_barrier_semaphore()
    entered = [after, before, sibling] + along_x + along_y + along_z
    greet(barrier, entered)
    pl.semaphore_wait(barrier, len(entered))

    rounds = [
        ((meet.at[0], along_x), (meet.at[1], along_z)),
        ((meet.at[2], along_y), (meet.at[3], along_z)),
        ((meet.at[4], along_y), (meet.at[5], along_z)),
        ((meet.at[6], [sibling]),),
    ]

    def announce(n):
        for semaphore, targets in rounds[n]:
            greet(semaphore, targets)

    def learn(n):
        for semaphore, targets in rounds[n]:
            pl.semaphore_wait(semaphore, len(targets))

    halo = {}
    waited = set()
    for t in range(8):
        for which, c, target in ((0, 7 - t, after), (1, t, before)):
            if c not in waited:
                own_copies[c].wait()
                waited.add(c)
            halo[which, t] = remote(
                own.at[core, c], landing.at[which, c, core],
                halo_send.at[which, c], halo_recv.at[which, c], target,
            )
            halo[which, t].start()
    share = remote(own.at[core], own.at[core], share_send, share_recv, sibling)
    share.start()
    announce(0)

    def mine(n):
        return (1 - core) * (3 - n) + core * (4 + n)

    def block_copy(c):
        return pltpu.make_async_copy(blocks_ref.at[c], blocks.at[c], block_sem.at[c])

    for c in (3, 4, 2, 5, 1, 6, 0, 7):
        block_copy(c).start()
    share.wait_recv()
    for c in range(8):
        for half in range(2):
            window[8 + c, half * K:(half + 1) * K, :] = own[half, c]

    passed, parts, tiles = {}, {}, {}

    def absorb(t):
        for which, c in ((0, 7 - t), (1, t)):
            passed[which, t].wait_recv()
            for half in range(2):
                window[16 * which + c, half * K:(half + 1) * K, :] = landing[which, c, half]

    def product(c):
        acc = jnp.zeros((LEAF, LEAF), jnp.float32)
        for b in range(8):
            at = jnp.clip(cols_ref[c, b] - (row * 8 - 8), 0, 23)
            acc = acc + cross(window[at], blocks[c, b])
        return acc

    def multiply(n):
        block_copy(3 - n).wait()
        block_copy(4 + n).wait()
        given[n] = product(7 - mine(n))
        parts[n] = remote(given.at[n], theirs.at[n], part_send.at[n], part_recv.at[n], sibling)
        parts[n].start()
        kept[n] = product(mine(n))

    def sample_out(n, c):
        at = pl.multiple_of(c * LEAF, LEAF)
        return pltpu.make_async_copy(stage.at[c], sample_ref.at[:, pl.ds(at, LEAF)], out_sem.at[n])

    def finish(n):
        c = mine(n)
        parts[n].wait_recv()
        full = kept[n] + theirs[n]
        kept[n] = full
        gram = cross(full[:K], full, HIGH)
        leaf_a[n] = gram
        total[...] = gram if n == 0 else total[...] + gram

    def hand_out(n):
        c = mine(n)
        stage[c] = kept[n, pl.ds(pl.multiple_of(core * K, K), K), :].astype(jnp.bfloat16)
        sent_stage[n] = kept[n, pl.ds(pl.multiple_of((1 - core) * K, K), K), :].astype(jnp.bfloat16)
        tiles[n] = remote(sent_stage.at[n], stage.at[c], tile_send.at[n], tile_recv.at[n], sibling)
        tiles[n].start()
        sample_out(n, c).start()

    for t in range(9):
        if t < 8:
            for which, c in ((0, 7 - t), (1, t)):
                halo[which, t].wait_recv()
                passed[which, t] = remote(
                    landing.at[which, c, core], landing.at[which, c, core],
                    pass_send.at[which, c], pass_recv.at[which, c], sibling,
                )
                passed[which, t].start()
        if t >= 1:
            absorb(t - 1)
        if 1 <= t <= 4:
            learn(t - 1)
            if t < 4:
                announce(t)
        if t >= 5:
            multiply(t - 5)
        if t >= 6:
            finish(t - 6)
            if t < 8:
                hand_out(t - 6)
    finish(3)

    def scatter(step):
        at = pl.multiple_of(lax.rem(spot + step, PLANE) * 8, 8)
        return remote(total.at[pl.ds(at, 8), :], rs_buf.at[step], rs_send.at[step], rs_recv.at[step], in_plane(step))

    def column(step):
        return remote(z_buf.at[0], z_buf.at[step], z_send.at[step], z_recv.at[step], in_column(step))

    here = pl.ds(pl.multiple_of(spot * 8, 8), 8)

    def publish(step):
        return remote(root_ref.at[here, :], root_ref.at[here, :], ag_send.at[step], ag_recv.at[step], in_plane(step))

    def published(step):
        place = pl.ds(pl.multiple_of(lax.rem(spot + PLANE - step, PLANE) * 8, 8), 8)
        return remote(root_ref.at[place, :], root_ref.at[place, :], ag_send.at[step], ag_recv.at[step], in_plane(step))

    def each(count, act):
        def body(step, carry):
            act(step)
            return carry

        lax.fori_loop(1, count, body, 0)

    each(PLANE, lambda step: scatter(step).start())
    rs_buf[0] = total[here, :]
    hand_out(2)
    hand_out(3)
    t0[...] = jnp.zeros_like(t0)
    t1[...] = jnp.zeros_like(t1)
    for k in range(0, 3):
        factor_panel(leaf_a, 4, t0, t1, k)
    each(PLANE, lambda step: scatter(step).wait())
    z_buf[0] = jnp.sum(rs_buf[...], axis=0)
    each(2 * depth, lambda step: column(step).start())
    for n in range(4):
        tiles[n].wait_recv()
        sample_out(4 + n, 7 - mine(n)).start()
    for k in range(3, 6):
        factor_panel(leaf_a, 4, t0, t1, k)
    each(2 * depth, lambda step: column(step).wait())
    root_ref[here, :] = jnp.sum(z_buf[...], axis=0)
    each(PLANE, lambda step: publish(step).start())
    for k in range(6, 8):
        factor_panel(leaf_a, 4, t0, t1, k)
    leaves = []
    for n in range(4):
        sent_leaf[n] = leaf_a[n, :, pl.ds(pl.multiple_of((1 - core) * K, K), K)].T
        leaves.append(remote(sent_leaf.at[n], leaf_buf.at[mine(n)], leaf_send.at[n], leaf_recv.at[n], sibling))
        leaves[n].start()
        leaf_buf[mine(n)] = leaf_a[n, :, pl.ds(pl.multiple_of(core * K, K), K)].T
    for n in range(4):
        leaves[n].wait_recv()
    leaf_out = pltpu.make_async_copy(leaf_buf, leaf_ref, leaf_sem)
    leaf_out.start()

    def close(step):
        publish(step).wait_send()
        published(step).wait_recv()

    each(PLANE, close)
    share.wait_send()
    for copy in list(halo.values()) + list(passed.values()) + list(parts.values()) + list(tiles.values()) + leaves:
        copy.wait_send()
    for n in range(4):
        sample_out(n, mine(n)).wait()
        sample_out(4 + n, 7 - mine(n)).wait()
    leaf_out.wait()


def gather(block_cols, probe_matrix, near_blocks):
    depth = lax.axis_size("rows") // PLANE
    bf16, f32, dma = jnp.bfloat16, jnp.float32, pltpu.SemaphoreType.DMA
    hbm = pl.BlockSpec(memory_space=pltpu.HBM)
    return pl.pallas_call(
        functools.partial(gather_kernel, depth),
        out_shape=(
            jax.ShapeDtypeStruct((K, 8 * LEAF), bf16),
            jax.ShapeDtypeStruct((8, K, K), f32),
            jax.ShapeDtypeStruct((K, LEAF), f32),
        ),
        in_specs=[pl.BlockSpec(memory_space=pltpu.SMEM), hbm, hbm],
        out_specs=(hbm, hbm, pl.BlockSpec(memory_space=pltpu.VMEM)),
        scratch_shapes=[
            pltpu.VMEM((2, 8, K, LEAF), bf16),
            pltpu.VMEM((2, 8, 2, K, LEAF), bf16),
            pltpu.VMEM((24, LEAF, LEAF), bf16),
            pltpu.VMEM((8, 8, LEAF, LEAF), bf16),
            pltpu.VMEM((4, LEAF, LEAF), f32),
            pltpu.VMEM((4, LEAF, LEAF), f32),
            pltpu.VMEM((4, LEAF, LEAF), f32),
            pltpu.VMEM((8, K, LEAF), bf16),
            pltpu.VMEM((4, K, LEAF), bf16),
            pltpu.VMEM((K, LEAF), f32),
            pltpu.VMEM((PLANE, 8, LEAF), f32),
            pltpu.VMEM((2 * depth, 8, LEAF), f32),
            pltpu.VMEM((4, K, 2 * K), f32),
            pltpu.VMEM((PANEL * SUB, K), f32),
            pltpu.VMEM((PANEL * SUB, K), f32),
            pltpu.VMEM((8, K, K), f32),
            pltpu.VMEM((4, K, K), f32),
            pltpu.SemaphoreType.REGULAR((7,)),
            dma((8,)), dma((8,)), dma, dma, dma((2, 8)), dma((2, 8)), dma((2, 8)), dma((2, 8)),
            dma((4,)), dma((4,)), dma((4,)), dma((4,)), dma((8,)), dma((4,)), dma((4,)), dma,
            dma((PLANE,)), dma((PLANE,)), dma((2 * depth,)), dma((2 * depth,)), dma((PLANE,)), dma((PLANE,)),
        ],
        compiler_params=pltpu.CompilerParams(
            collective_id=0, has_side_effects=True, vmem_limit_bytes=56 * 2**20
        ),
        name="gather",
    )(block_cols, probe_matrix, near_blocks)


def factor_kernel(c_ref, sample_in, leaf_in, sample_ref, leaf_ref, out_ref, r_ref, f_ref, t0, t1, sems):
    copies = [
        pltpu.make_async_copy(sample_in, sample_ref, sems.at[0]),
        pltpu.make_async_copy(leaf_in, leaf_ref, sems.at[1]),
    ]
    for copy in copies:
        copy.start()
    r_ref[0] = c_ref[...]
    for k in range(K // PANEL):
        factor_panel(r_ref, 1, t0, t1, k)
    f_ref[...] = r_ref[0].T
    out_ref[...] = f_ref[pl.ds(lax.axis_index("rows") * 2 + lax.axis_index("probe"), 1), :]
    for copy in copies:
        copy.wait()


def factor(root_gram, sample, leaf):
    whole, hbm = pl.BlockSpec(memory_space=pltpu.VMEM), pl.BlockSpec(memory_space=pltpu.HBM)
    rows = pltpu.VMEM((PANEL * SUB, K), jnp.float32)
    return pl.pallas_call(
        factor_kernel,
        out_shape=(
            jax.ShapeDtypeStruct(sample.shape, sample.dtype),
            jax.ShapeDtypeStruct(leaf.shape, leaf.dtype),
            jax.ShapeDtypeStruct((1, K), jnp.float32),
        ),
        in_specs=[whole, hbm, hbm],
        out_specs=(hbm, hbm, whole),
        scratch_shapes=[
            pltpu.VMEM((1, K, 2 * K), jnp.float32),
            pltpu.VMEM((2 * K, K), jnp.float32),
            rows, rows, pltpu.SemaphoreType.DMA((2,)),
        ],
        name="factor",
    )(root_gram, sample, leaf)


def local(probe_matrix, near_blocks, block_cols):
    sample, leaf, root_gram = gather(block_cols, probe_matrix, near_blocks)
    return factor(root_gram, sample, leaf)


def solution(mesh):
    placed = (P("probe", "rows"), P("rows", "probe", None, None), P("rows", "probe"))
    return jax.shard_map(
        local,
        mesh=mesh,
        in_specs=placed,
        out_specs=(P("probe", "rows"), P("rows", "probe", None), P(("rows", "probe"), None)),
        check_vma=False,
    )
```

```python
import functools

import jax
import jax.numpy as jnp
from jax import lax
from jax.experimental import pallas as pl
from jax.experimental.pallas import tpu as pltpu
from jax.sharding import PartitionSpec as P

K = 128
LEAF = 256
PLANE = 16
PANEL = 16
BLOCK = 8
SUB = 8
HIGH = lax.Precision.HIGHEST
MESH = pl.DeviceIdType.MESH


def cross(a, b, precision=None):
    return lax.dot_general(
        a, b, (((1,), (1,)), ((), ())), precision=precision, preferred_element_type=jnp.float32
    )


def eliminate_block(rows, c0):
    e = {}
    for j in range(BLOCK):
        for i in range(j, BLOCK):
            e[j, i] = jnp.broadcast_to(rows[j][0][:, c0 + i:c0 + i + 1], (SUB, K))
    for j in range(BLOCK):
        rs = lax.rsqrt(e[j, j])
        f = {i: e[j, i] * rs for i in range(j + 1, BLOCK)}
        rows[j] = [h * rs for h in rows[j]]
        for i in range(j + 1, BLOCK):
            for i2 in range(i, BLOCK):
                e[i, i2] = e[i, i2] - f[i] * f[i2]
            rows[i] = [h - f[i] * p for h, p in zip(rows[i], rows[j])]
    for i in range(BLOCK, len(rows)):
        for j in range(BLOCK):
            f = jnp.broadcast_to(rows[j][0][:, c0 + i:c0 + i + 1], (SUB, K))
            rows[i] = [h - f * p for h, p in zip(rows[i], rows[j])]
    return rows


def factor_panel(a_ref, count, t0, t1, k):
    r0 = k * PANEL
    lane = lax.broadcasted_iota(jnp.int32, (PANEL, K), 1)
    sub = lax.broadcasted_iota(jnp.int32, (PANEL, K), 0)
    if count == 1:
        rows = [
            [jnp.broadcast_to(a_ref[0, r0 + r:r0 + r + 1, h * K:(h + 1) * K], (SUB, K)) for h in range(2)]
            for r in range(PANEL)
        ]
    else:
        for s in range(count):
            t0[pl.ds(s, PANEL, stride=SUB), :] = a_ref[s, r0:r0 + PANEL, 0:K]
            t1[pl.ds(s, PANEL, stride=SUB), :] = a_ref[s, r0:r0 + PANEL, K:2 * K]
        rows = [[t[SUB * r:SUB * r + SUB, :] for t in (t0, t1)] for r in range(PANEL)]
    for c in range(0, PANEL, BLOCK):
        rows = rows[:c] + eliminate_block(rows[c:], r0 + c)
    for r in range(PANEL):
        t0[SUB * r:SUB * r + SUB, :] = rows[r][0]
        t1[SUB * r:SUB * r + SUB, :] = rows[r][1]
    for s in range(count):
        low = jnp.where(lane >= r0 + sub, t0[pl.ds(s, PANEL, stride=SUB), :], 0.0)
        high = t1[pl.ds(s, PANEL, stride=SUB), :]
        a_ref[s, r0:r0 + PANEL, 0:K] = low
        a_ref[s, r0:r0 + PANEL, K:2 * K] = high
        if r0 + PANEL < K:
            left = low.T[r0 + PANEL:, :]
            right = jnp.concatenate([low, high], axis=1)
            a_ref[s, r0 + PANEL:, :] = a_ref[s, r0 + PANEL:, :] - jnp.dot(
                left, right, precision=HIGH, preferred_element_type=jnp.float32
            )


def gather_kernel(
    depth, cols_ref, probe_ref, blocks_ref,
    sample_ref, leaf_ref, root_ref,
    own, landing, window, blocks, given, kept, theirs, stage, sent_stage, total, rs_buf, z_buf,
    leaf_a, t0, t1, leaf_buf, sent_leaf,
    meet, block_sem, own_sem, share_send, share_recv, halo_send, halo_recv, pass_send, pass_recv,
    part_send, part_recv, tile_send, tile_recv, out_sem, leaf_send, leaf_recv, leaf_sem,
    rs_send, rs_recv, z_send, z_recv, ag_send, ag_recv,
):
    row, core = lax.axis_index("rows"), lax.axis_index("probe")
    rows = PLANE * depth
    sibling = (row, 1 - core)
    after, before = (lax.rem(row + 1, rows), core), (lax.rem(row + rows - 1, rows), core)
    layer, spot = row // PLANE, lax.rem(row, PLANE)
    side, front = lax.rem(spot, 4), spot // 4

    def in_plane(step):
        return (layer * PLANE + lax.rem(spot + step, PLANE), core)

    def in_column(step):
        return (lax.rem(layer + step, depth) * PLANE + spot, lax.rem(core + step // depth, 2))

    along_x = [(layer * PLANE + front * 4 + lax.rem(side + d, 4), core) for d in (1, 3)]
    along_y = [in_plane(4), in_plane(12)]
    along_z = [in_column(1), in_column(depth - 1)]

    def greet(semaphore, targets):
        for target in targets:
            pl.semaphore_signal(semaphore, inc=1, device_id=target, device_id_type=MESH)

    def remote(src, dst, send, recv, target):
        return pltpu.make_async_remote_copy(
            src_ref=src, dst_ref=dst, send_sem=send, recv_sem=recv,
            device_id=target, device_id_type=MESH,
        )

    own_copies = {}
    for c in (7, 0, 6, 1, 5, 2, 4, 3):
        own_copies[c] = pltpu.make_async_copy(
            probe_ref.at[:, c * LEAF:(c + 1) * LEAF], own.at[core, c], own_sem.at[c]
        )
        own_copies[c].start()
    barrier = pltpu.get_barrier_semaphore()
    entered = [after, before, sibling] + along_x + along_y + along_z
    greet(barrier, entered)
    pl.semaphore_wait(barrier, len(entered))

    rounds = [
        ((meet.at[0], along_x), (meet.at[1], along_z)),
        ((meet.at[2], along_y), (meet.at[3], along_z)),
        ((meet.at[4], along_y), (meet.at[5], along_z)),
        ((meet.at[6], [sibling]),),
    ]

    def announce(n):
        for semaphore, targets in rounds[n]:
            greet(semaphore, targets)

    def learn(n):
        for semaphore, targets in rounds[n]:
            pl.semaphore_wait(semaphore, len(targets))

    halo = {}
    waited = set()
    for t in range(8):
        for which, c, target in ((0, 7 - t, after), (1, t, before)):
            if c not in waited:
                own_copies[c].wait()
                waited.add(c)
            halo[which, t] = remote(
                own.at[core, c], landing.at[which, c, core],
                halo_send.at[which, c], halo_recv.at[which, c], target,
            )
            halo[which, t].start()
    share = remote(own.at[core], own.at[core], share_send, share_recv, sibling)
    share.start()
    announce(0)

    def mine(n):
        return (1 - core) * (3 - n) + core * (4 + n)

    def block_copy(c):
        return pltpu.make_async_copy(blocks_ref.at[c], blocks.at[c], block_sem.at[c])

    for c in (3, 4, 2, 5, 1, 6, 0, 7):
        block_copy(c).start()
    share.wait_recv()
    for c in range(8):
        for half in range(2):
            window[8 + c, half * K:(half + 1) * K, :] = own[half, c]

    passed, parts, tiles = {}, {}, {}

    def absorb(t):
        for which, c in ((0, 7 - t), (1, t)):
            passed[which, t].wait_recv()
            for half in range(2):
                window[16 * which + c, half * K:(half + 1) * K, :] = landing[which, c, half]

    def product(c):
        acc = jnp.zeros((LEAF, LEAF), jnp.float32)
        for b in range(8):
            at = jnp.clip(cols_ref[c, b] - (row * 8 - 8), 0, 23)
            acc = acc + cross(window[at], blocks[c, b])
        return acc

    def multiply(n):
        block_copy(3 - n).wait()
        block_copy(4 + n).wait()
        given[n] = product(7 - mine(n))
        parts[n] = remote(given.at[n], theirs.at[n], part_send.at[n], part_recv.at[n], sibling)
        parts[n].start()
        kept[n] = product(mine(n))

    def sample_out(n, c):
        at = pl.multiple_of(c * LEAF, LEAF)
        return pltpu.make_async_copy(stage.at[c], sample_ref.at[:, pl.ds(at, LEAF)], out_sem.at[n])

    def finish(n):
        c = mine(n)
        parts[n].wait_recv()
        full = kept[n] + theirs[n]
        kept[n] = full
        gram = cross(full[:K], full, HIGH)
        leaf_a[n] = gram
        total[...] = gram if n == 0 else total[...] + gram

    def hand_out(n):
        c = mine(n)
        stage[c] = kept[n, pl.ds(pl.multiple_of(core * K, K), K), :].astype(jnp.bfloat16)
        sent_stage[n] = kept[n, pl.ds(pl.multiple_of((1 - core) * K, K), K), :].astype(jnp.bfloat16)
        tiles[n] = remote(sent_stage.at[n], stage.at[c], tile_send.at[n], tile_recv.at[n], sibling)
        tiles[n].start()
        sample_out(n, c).start()

    for t in range(9):
        if t < 8:
            for which, c in ((0, 7 - t), (1, t)):
                halo[which, t].wait_recv()
                passed[which, t] = remote(
                    landing.at[which, c, core], landing.at[which, c, core],
                    pass_send.at[which, c], pass_recv.at[which, c], sibling,
                )
                passed[which, t].start()
        if t >= 1:
            absorb(t - 1)
        if 1 <= t <= 4:
            learn(t - 1)
            if t < 4:
                announce(t)
        if t >= 5:
            multiply(t - 5)
        if t >= 6:
            finish(t - 6)
            if t < 8:
                hand_out(t - 6)
    finish(3)

    def scatter(step):
        at = pl.multiple_of(lax.rem(spot + step, PLANE) * 8, 8)
        return remote(total.at[pl.ds(at, 8), :], rs_buf.at[step], rs_send.at[step], rs_recv.at[step], in_plane(step))

    def column(step):
        return remote(z_buf.at[0], z_buf.at[step], z_send.at[step], z_recv.at[step], in_column(step))

    here = pl.ds(pl.multiple_of(spot * 8, 8), 8)

    def publish(step):
        return remote(root_ref.at[here, :], root_ref.at[here, :], ag_send.at[step], ag_recv.at[step], in_plane(step))

    def published(step):
        place = pl.ds(pl.multiple_of(lax.rem(spot + PLANE - step, PLANE) * 8, 8), 8)
        return remote(root_ref.at[place, :], root_ref.at[place, :], ag_send.at[step], ag_recv.at[step], in_plane(step))

    def each(count, act):
        def body(step, carry):
            act(step)
            return carry

        lax.fori_loop(1, count, body, 0)

    each(PLANE, lambda step: scatter(step).start())
    rs_buf[0] = total[here, :]
    hand_out(2)
    hand_out(3)
    t0[...] = jnp.zeros_like(t0)
    t1[...] = jnp.zeros_like(t1)
    for k in range(0, 3):
        factor_panel(leaf_a, 4, t0, t1, k)
    each(PLANE, lambda step: scatter(step).wait())
    z_buf[0] = jnp.sum(rs_buf[...], axis=0)
    each(2 * depth, lambda step: column(step).start())
    for n in range(4):
        tiles[n].wait_recv()
        sample_out(4 + n, 7 - mine(n)).start()
    for k in range(3, 6):
        factor_panel(leaf_a, 4, t0, t1, k)
    each(2 * depth, lambda step: column(step).wait())
    root_ref[here, :] = jnp.sum(z_buf[...], axis=0)
    each(PLANE, lambda step: publish(step).start())
    for k in range(6, 8):
        factor_panel(leaf_a, 4, t0, t1, k)
    leaves = []
    for n in range(4):
        sent_leaf[n] = leaf_a[n, :, pl.ds(pl.multiple_of((1 - core) * K, K), K)].T
        leaves.append(remote(sent_leaf.at[n], leaf_buf.at[mine(n)], leaf_send.at[n], leaf_recv.at[n], sibling))
        leaves[n].start()
        leaf_buf[mine(n)] = leaf_a[n, :, pl.ds(pl.multiple_of(core * K, K), K)].T
    for n in range(4):
        leaves[n].wait_recv()
    leaf_out = pltpu.make_async_copy(leaf_buf, leaf_ref, leaf_sem)
    leaf_out.start()

    def close(step):
        publish(step).wait_send()
        published(step).wait_recv()

    each(PLANE, close)
    share.wait_send()
    for copy in list(halo.values()) + list(passed.values()) + list(parts.values()) + list(tiles.values()) + leaves:
        copy.wait_send()
    for n in range(4):
        sample_out(n, mine(n)).wait()
        sample_out(4 + n, 7 - mine(n)).wait()
    leaf_out.wait()


def gather(block_cols, probe_matrix, near_blocks):
    depth = lax.axis_size("rows") // PLANE
    bf16, f32, dma = jnp.bfloat16, jnp.float32, pltpu.SemaphoreType.DMA
    hbm = pl.BlockSpec(memory_space=pltpu.HBM)
    return pl.pallas_call(
        functools.partial(gather_kernel, depth),
        out_shape=(
            jax.ShapeDtypeStruct((K, 8 * LEAF), bf16),
            jax.ShapeDtypeStruct((8, K, K), f32),
            jax.ShapeDtypeStruct((K, LEAF), f32),
        ),
        in_specs=[pl.BlockSpec(memory_space=pltpu.SMEM), hbm, hbm],
        out_specs=(hbm, hbm, pl.BlockSpec(memory_space=pltpu.VMEM)),
        scratch_shapes=[
            pltpu.VMEM((2, 8, K, LEAF), bf16),
            pltpu.VMEM((2, 8, 2, K, LEAF), bf16),
            pltpu.VMEM((24, LEAF, LEAF), bf16),
            pltpu.VMEM((8, 8, LEAF, LEAF), bf16),
            pltpu.VMEM((4, LEAF, LEAF), f32),
            pltpu.VMEM((4, LEAF, LEAF), f32),
            pltpu.VMEM((4, LEAF, LEAF), f32),
            pltpu.VMEM((8, K, LEAF), bf16),
            pltpu.VMEM((4, K, LEAF), bf16),
            pltpu.VMEM((K, LEAF), f32),
            pltpu.VMEM((PLANE, 8, LEAF), f32),
            pltpu.VMEM((2 * depth, 8, LEAF), f32),
            pltpu.VMEM((4, K, 2 * K), f32),
            pltpu.VMEM((PANEL * SUB, K), f32),
            pltpu.VMEM((PANEL * SUB, K), f32),
            pltpu.VMEM((8, K, K), f32),
            pltpu.VMEM((4, K, K), f32),
            pltpu.SemaphoreType.REGULAR((7,)),
            dma((8,)), dma((8,)), dma, dma, dma((2, 8)), dma((2, 8)), dma((2, 8)), dma((2, 8)),
            dma((4,)), dma((4,)), dma((4,)), dma((4,)), dma((8,)), dma((4,)), dma((4,)), dma,
            dma((PLANE,)), dma((PLANE,)), dma((2 * depth,)), dma((2 * depth,)), dma((PLANE,)), dma((PLANE,)),
        ],
        compiler_params=pltpu.CompilerParams(
            collective_id=0, has_side_effects=True, vmem_limit_bytes=56 * 2**20
        ),
        name="gather",
    )(block_cols, probe_matrix, near_blocks)


def factor_kernel(c_ref, sample_in, leaf_in, sample_ref, leaf_ref, out_ref, r_ref, f_ref, t0, t1, sample_v, leaf_v, sems):
    inward = [
        pltpu.make_async_copy(sample_in, sample_v, sems.at[0]),
        pltpu.make_async_copy(leaf_in, leaf_v, sems.at[1]),
    ]
    outward = [
        pltpu.make_async_copy(sample_v, sample_ref, sems.at[2]),
        pltpu.make_async_copy(leaf_v, leaf_ref, sems.at[3]),
    ]
    for copy in inward:
        copy.start()
    r_ref[0] = c_ref[...]
    for k in range(K // PANEL):
        factor_panel(r_ref, 1, t0, t1, k)
        if k == 3:
            for copy in inward:
                copy.wait()
            for copy in outward:
                copy.start()
    f_ref[...] = r_ref[0].T
    out_ref[...] = f_ref[pl.ds(lax.axis_index("rows") * 2 + lax.axis_index("probe"), 1), :]
    for copy in outward:
        copy.wait()


def factor(root_gram, sample, leaf):
    whole, hbm = pl.BlockSpec(memory_space=pltpu.VMEM), pl.BlockSpec(memory_space=pltpu.HBM)
    rows = pltpu.VMEM((PANEL * SUB, K), jnp.float32)
    return pl.pallas_call(
        factor_kernel,
        out_shape=(
            jax.ShapeDtypeStruct(sample.shape, sample.dtype),
            jax.ShapeDtypeStruct(leaf.shape, leaf.dtype),
            jax.ShapeDtypeStruct((1, K), jnp.float32),
        ),
        in_specs=[whole, hbm, hbm],
        out_specs=(hbm, hbm, whole),
        scratch_shapes=[
            pltpu.VMEM((1, K, 2 * K), jnp.float32),
            pltpu.VMEM((2 * K, K), jnp.float32),
            rows, rows,
            pltpu.VMEM(sample.shape, sample.dtype),
            pltpu.VMEM(leaf.shape, leaf.dtype),
            pltpu.SemaphoreType.DMA((4,)),
        ],
        name="factor",
    )(root_gram, sample, leaf)


def local(probe_matrix, near_blocks, block_cols):
    sample, leaf, root_gram = gather(block_cols, probe_matrix, near_blocks)
    return factor(root_gram, sample, leaf)


def solution(mesh):
    placed = (P("probe", "rows"), P("rows", "probe", None, None), P("rows", "probe"))
    return jax.shard_map(
        local,
        mesh=mesh,
        in_specs=placed,
        out_specs=(P("probe", "rows"), P("rows", "probe", None), P(("rows", "probe"), None)),
        check_vma=False,
    )
```

```python
import functools

import jax
import jax.numpy as jnp
from jax import lax
from jax.experimental import pallas as pl
from jax.experimental.pallas import tpu as pltpu
from jax.sharding import PartitionSpec as P

K = 128
LEAF = 256
PLANE = 16
PANEL = 16
BLOCK = 8
SUB = 8
HIGH = lax.Precision.HIGHEST
MESH = pl.DeviceIdType.MESH


def cross(a, b, precision=None):
    return lax.dot_general(
        a, b, (((1,), (1,)), ((), ())), precision=precision, preferred_element_type=jnp.float32
    )


def eliminate_block(rows, c0):
    e = {}
    for j in range(BLOCK):
        for i in range(j, BLOCK):
            e[j, i] = jnp.broadcast_to(rows[j][0][:, c0 + i:c0 + i + 1], (SUB, K))
    for j in range(BLOCK):
        rs = lax.rsqrt(e[j, j])
        f = {i: e[j, i] * rs for i in range(j + 1, BLOCK)}
        rows[j] = [h * rs for h in rows[j]]
        for i in range(j + 1, BLOCK):
            for i2 in range(i, BLOCK):
                e[i, i2] = e[i, i2] - f[i] * f[i2]
            rows[i] = [h - f[i] * p for h, p in zip(rows[i], rows[j])]
    for i in range(BLOCK, len(rows)):
        for j in range(BLOCK):
            f = jnp.broadcast_to(rows[j][0][:, c0 + i:c0 + i + 1], (SUB, K))
            rows[i] = [h - f * p for h, p in zip(rows[i], rows[j])]
    return rows


def factor_panel(a_ref, count, t0, t1, k):
    r0 = k * PANEL
    lane = lax.broadcasted_iota(jnp.int32, (PANEL, K), 1)
    sub = lax.broadcasted_iota(jnp.int32, (PANEL, K), 0)
    if count == 1:
        rows = [
            [jnp.broadcast_to(a_ref[0, r0 + r:r0 + r + 1, h * K:(h + 1) * K], (SUB, K)) for h in range(2)]
            for r in range(PANEL)
        ]
    else:
        for s in range(count):
            t0[pl.ds(s, PANEL, stride=SUB), :] = a_ref[s, r0:r0 + PANEL, 0:K]
            t1[pl.ds(s, PANEL, stride=SUB), :] = a_ref[s, r0:r0 + PANEL, K:2 * K]
        rows = [[t[SUB * r:SUB * r + SUB, :] for t in (t0, t1)] for r in range(PANEL)]
    for c in range(0, PANEL, BLOCK):
        rows = rows[:c] + eliminate_block(rows[c:], r0 + c)
    for r in range(PANEL):
        t0[SUB * r:SUB * r + SUB, :] = rows[r][0]
        t1[SUB * r:SUB * r + SUB, :] = rows[r][1]
    for s in range(count):
        low = jnp.where(lane >= r0 + sub, t0[pl.ds(s, PANEL, stride=SUB), :], 0.0)
        high = t1[pl.ds(s, PANEL, stride=SUB), :]
        a_ref[s, r0:r0 + PANEL, 0:K] = low
        a_ref[s, r0:r0 + PANEL, K:2 * K] = high
        if r0 + PANEL < K:
            left = low.T[r0 + PANEL:, :]
            right = jnp.concatenate([low, high], axis=1)
            a_ref[s, r0 + PANEL:, :] = a_ref[s, r0 + PANEL:, :] - jnp.dot(
                left, right, precision=HIGH, preferred_element_type=jnp.float32
            )


def gather_kernel(
    depth, cols_ref, probe_ref, blocks_ref,
    sample_ref, leaf_ref, root_ref,
    own, landing, window, blocks, given, kept, theirs, stage, sent_stage, total, rs_buf, z_buf,
    leaf_a, t0, t1, leaf_buf, sent_leaf,
    meet, block_sem, own_sem, share_send, share_recv, halo_send, halo_recv, pass_send, pass_recv,
    part_send, part_recv, tile_send, tile_recv, out_sem, leaf_send, leaf_recv, leaf_sem,
    rs_send, rs_recv, z_send, z_recv, ag_send, ag_recv,
):
    row, core = lax.axis_index("rows"), lax.axis_index("probe")
    rows = PLANE * depth
    sibling = (row, 1 - core)
    after, before = (lax.rem(row + 1, rows), core), (lax.rem(row + rows - 1, rows), core)
    layer, spot = row // PLANE, lax.rem(row, PLANE)
    side, front = lax.rem(spot, 4), spot // 4

    ring = [0, 1, 2, 1]
    plane_steps = sorted(
        [(dx, dy) for dx in range(4) for dy in range(4) if dx or dy], key=lambda d: -ring[d[0]] - ring[d[1]]
    )
    column_steps = sorted(
        [(dz, other) for dz in range(depth) for other in range(2) if dz or other],
        key=lambda d: -2 * min(d[0], depth - d[0]) - d[1],
    )
    xs = [lax.rem(side + d, 4) for d in range(4)]
    ys = [lax.rem(front + d, 4) for d in range(4)]
    zs = [lax.rem(layer + d, depth) for d in range(depth)]
    spots = {(dx, dy): ys[dy] * 4 + xs[dx] for dx in range(4) for dy in range(4)}

    def in_plane(step):
        return (layer * PLANE + spots[step], core)

    def in_column(step):
        return (zs[step[0]] * PLANE + spot, 1 - core if step[1] else core)

    def opposite(step):
        return ((4 - step[0]) % 4, (4 - step[1]) % 4)

    along_x = [in_plane((d, 0)) for d in (1, 3)]
    along_y = [in_plane((0, d)) for d in (1, 3)]
    along_z = [in_column((d, 0)) for d in (1, depth - 1)]

    def greet(semaphore, targets):
        for target in targets:
            pl.semaphore_signal(semaphore, inc=1, device_id=target, device_id_type=MESH)

    def remote(src, dst, send, recv, target):
        return pltpu.make_async_remote_copy(
            src_ref=src, dst_ref=dst, send_sem=send, recv_sem=recv,
            device_id=target, device_id_type=MESH,
        )

    own_copies = {}
    for c in (7, 0, 6, 1, 5, 2, 4, 3):
        own_copies[c] = pltpu.make_async_copy(
            probe_ref.at[:, c * LEAF:(c + 1) * LEAF], own.at[core, c], own_sem.at[c]
        )
        own_copies[c].start()
    barrier = pltpu.get_barrier_semaphore()
    entered = [after, before, sibling] + along_x + along_y + along_z
    greet(barrier, entered)
    pl.semaphore_wait(barrier, len(entered))

    rounds = [
        ((meet.at[0], along_x), (meet.at[1], along_z)),
        ((meet.at[2], along_y), (meet.at[3], along_z)),
        ((meet.at[4], along_y), (meet.at[5], along_z)),
        ((meet.at[6], [sibling]),),
    ]

    def announce(n):
        for semaphore, targets in rounds[n]:
            greet(semaphore, targets)

    def learn(n):
        for semaphore, targets in rounds[n]:
            pl.semaphore_wait(semaphore, len(targets))

    halo = {}
    waited = set()
    for t in range(8):
        for which, c, target in ((0, 7 - t, after), (1, t, before)):
            if c not in waited:
                own_copies[c].wait()
                waited.add(c)
            halo[which, t] = remote(
                own.at[core, c], landing.at[which, c, core],
                halo_send.at[which, c], halo_recv.at[which, c], target,
            )
            halo[which, t].start()
    share = remote(own.at[core], own.at[core], share_send, share_recv, sibling)
    share.start()
    announce(0)

    def mine(n):
        return (1 - core) * (3 - n) + core * (4 + n)

    def block_copy(c):
        return pltpu.make_async_copy(blocks_ref.at[c], blocks.at[c], block_sem.at[c])

    for c in (3, 4, 2, 5, 1, 6, 0, 7):
        block_copy(c).start()
    share.wait_recv()
    for c in range(8):
        for half in range(2):
            window[8 + c, half * K:(half + 1) * K, :] = own[half, c]

    passed, parts, tiles = {}, {}, {}

    def absorb(t):
        for which, c in ((0, 7 - t), (1, t)):
            passed[which, t].wait_recv()
            for half in range(2):
                window[16 * which + c, half * K:(half + 1) * K, :] = landing[which, c, half]

    def product(c):
        acc = jnp.zeros((LEAF, LEAF), jnp.float32)
        for b in range(8):
            at = jnp.clip(cols_ref[c, b] - (row * 8 - 8), 0, 23)
            acc = acc + cross(window[at], blocks[c, b])
        return acc

    def multiply(n):
        block_copy(3 - n).wait()
        block_copy(4 + n).wait()
        given[n] = product(7 - mine(n))
        parts[n] = remote(given.at[n], theirs.at[n], part_send.at[n], part_recv.at[n], sibling)
        parts[n].start()
        kept[n] = product(mine(n))

    def sample_out(n, c):
        at = pl.multiple_of(c * LEAF, LEAF)
        return pltpu.make_async_copy(stage.at[c], sample_ref.at[:, pl.ds(at, LEAF)], out_sem.at[n])

    def finish(n):
        c = mine(n)
        parts[n].wait_recv()
        full = kept[n] + theirs[n]
        kept[n] = full
        gram = cross(full[:K], full, HIGH)
        leaf_a[n] = gram
        total[...] = gram if n == 0 else total[...] + gram

    def hand_out(n):
        c = mine(n)
        stage[c] = kept[n, pl.ds(pl.multiple_of(core * K, K), K), :].astype(jnp.bfloat16)
        sent_stage[n] = kept[n, pl.ds(pl.multiple_of((1 - core) * K, K), K), :].astype(jnp.bfloat16)
        tiles[n] = remote(sent_stage.at[n], stage.at[c], tile_send.at[n], tile_recv.at[n], sibling)
        tiles[n].start()
        sample_out(n, c).start()

    for t in range(9):
        if t < 8:
            for which, c in ((0, 7 - t), (1, t)):
                halo[which, t].wait_recv()
                passed[which, t] = remote(
                    landing.at[which, c, core], landing.at[which, c, core],
                    pass_send.at[which, c], pass_recv.at[which, c], sibling,
                )
                passed[which, t].start()
        if t >= 1:
            absorb(t - 1)
        if 1 <= t <= 4:
            learn(t - 1)
            if t < 4:
                announce(t)
        if t >= 5:
            multiply(t - 5)
        if 6 <= t < 7:
            finish(0)
    finish(1)
    finish(2)
    finish(3)

    here = pl.ds(pl.multiple_of(spot * 8, 8), 8)
    pieces = {step: pl.ds(pl.multiple_of(spots[step] * 8, 8), 8) for step in plane_steps}

    scatters = [
        remote(
            total.at[pieces[step], :], rs_buf.at[step[1] * 4 + step[0]],
            rs_send.at[step[1] * 4 + step[0]], rs_recv.at[step[1] * 4 + step[0]], in_plane(step),
        )
        for step in plane_steps
    ]
    for copy in scatters:
        copy.start()
    rs_buf[0] = total[here, :]
    for n in range(4):
        hand_out(n)
    t0[...] = jnp.zeros_like(t0)
    t1[...] = jnp.zeros_like(t1)
    for k in range(0, 3):
        factor_panel(leaf_a, 4, t0, t1, k)
    for copy in scatters:
        copy.wait_recv()
    z_buf[0] = jnp.sum(rs_buf[...], axis=0)

    columns = [
        remote(
            z_buf.at[0], z_buf.at[step[0] * 2 + step[1]],
            z_send.at[step[0] * 2 + step[1]], z_recv.at[step[0] * 2 + step[1]], in_column(step),
        )
        for step in column_steps
    ]
    for copy in columns:
        copy.start()
    for copy in scatters:
        copy.wait_send()
    for n in range(4):
        tiles[n].wait_recv()
        sample_out(4 + n, 7 - mine(n)).start()
    for k in range(3, 6):
        factor_panel(leaf_a, 4, t0, t1, k)
    for copy in columns:
        copy.wait_recv()
    root_ref[here, :] = jnp.sum(z_buf[...], axis=0)

    def publish(place, step):
        at = step[1] * 4 + step[0]
        return remote(root_ref.at[place, :], root_ref.at[place, :], ag_send.at[at], ag_recv.at[at], in_plane(step))

    published = [publish(here, step) for step in plane_steps]
    for copy in published:
        copy.start()
    for copy in columns:
        copy.wait_send()
    for k in range(6, 8):
        factor_panel(leaf_a, 4, t0, t1, k)
    leaves = []
    for n in range(4):
        sent_leaf[n] = leaf_a[n, :, pl.ds(pl.multiple_of((1 - core) * K, K), K)].T
        leaves.append(remote(sent_leaf.at[n], leaf_buf.at[mine(n)], leaf_send.at[n], leaf_recv.at[n], sibling))
        leaves[n].start()
        leaf_buf[mine(n)] = leaf_a[n, :, pl.ds(pl.multiple_of(core * K, K), K)].T
    for n in range(4):
        leaves[n].wait_recv()
    leaf_out = pltpu.make_async_copy(leaf_buf, leaf_ref, leaf_sem)
    leaf_out.start()
    for copy in published:
        copy.wait_send()
    for step in plane_steps:
        publish(pieces[opposite(step)], step).wait_recv()
    share.wait_send()
    for copy in list(halo.values()) + list(passed.values()) + list(parts.values()) + list(tiles.values()) + leaves:
        copy.wait_send()
    for n in range(4):
        sample_out(n, mine(n)).wait()
        sample_out(4 + n, 7 - mine(n)).wait()
    leaf_out.wait()


def gather(block_cols, probe_matrix, near_blocks):
    depth = lax.axis_size("rows") // PLANE
    bf16, f32, dma = jnp.bfloat16, jnp.float32, pltpu.SemaphoreType.DMA
    hbm = pl.BlockSpec(memory_space=pltpu.HBM)
    return pl.pallas_call(
        functools.partial(gather_kernel, depth),
        out_shape=(
            jax.ShapeDtypeStruct((K, 8 * LEAF), bf16),
            jax.ShapeDtypeStruct((8, K, K), f32),
            jax.ShapeDtypeStruct((K, LEAF), f32),
        ),
        in_specs=[pl.BlockSpec(memory_space=pltpu.SMEM), hbm, hbm],
        out_specs=(hbm, hbm, pl.BlockSpec(memory_space=pltpu.VMEM)),
        scratch_shapes=[
            pltpu.VMEM((2, 8, K, LEAF), bf16),
            pltpu.VMEM((2, 8, 2, K, LEAF), bf16),
            pltpu.VMEM((24, LEAF, LEAF), bf16),
            pltpu.VMEM((8, 8, LEAF, LEAF), bf16),
            pltpu.VMEM((4, LEAF, LEAF), f32),
            pltpu.VMEM((4, LEAF, LEAF), f32),
            pltpu.VMEM((4, LEAF, LEAF), f32),
            pltpu.VMEM((8, K, LEAF), bf16),
            pltpu.VMEM((4, K, LEAF), bf16),
            pltpu.VMEM((K, LEAF), f32),
            pltpu.VMEM((PLANE, 8, LEAF), f32),
            pltpu.VMEM((2 * depth, 8, LEAF), f32),
            pltpu.VMEM((4, K, 2 * K), f32),
            pltpu.VMEM((PANEL * SUB, K), f32),
            pltpu.VMEM((PANEL * SUB, K), f32),
            pltpu.VMEM((8, K, K), f32),
            pltpu.VMEM((4, K, K), f32),
            pltpu.SemaphoreType.REGULAR((7,)),
            dma((8,)), dma((8,)), dma, dma, dma((2, 8)), dma((2, 8)), dma((2, 8)), dma((2, 8)),
            dma((4,)), dma((4,)), dma((4,)), dma((4,)), dma((8,)), dma((4,)), dma((4,)), dma,
            dma((PLANE,)), dma((PLANE,)), dma((2 * depth,)), dma((2 * depth,)), dma((PLANE,)), dma((PLANE,)),
        ],
        compiler_params=pltpu.CompilerParams(
            collective_id=0, has_side_effects=True, vmem_limit_bytes=56 * 2**20
        ),
        name="gather",
    )(block_cols, probe_matrix, near_blocks)


def factor_kernel(c_ref, sample_in, leaf_in, sample_ref, leaf_ref, out_ref, r_ref, f_ref, t0, t1, sample_v, leaf_v, sems):
    inward = [
        pltpu.make_async_copy(sample_in, sample_v, sems.at[0]),
        pltpu.make_async_copy(leaf_in, leaf_v, sems.at[1]),
    ]
    outward = [
        pltpu.make_async_copy(sample_v, sample_ref, sems.at[2]),
        pltpu.make_async_copy(leaf_v, leaf_ref, sems.at[3]),
    ]
    for copy in inward:
        copy.start()
    r_ref[0] = c_ref[...]
    for k in range(K // PANEL):
        factor_panel(r_ref, 1, t0, t1, k)
        if k == 3:
            for copy in inward:
                copy.wait()
            for copy in outward:
                copy.start()
    f_ref[...] = r_ref[0].T
    out_ref[...] = f_ref[pl.ds(lax.axis_index("rows") * 2 + lax.axis_index("probe"), 1), :]
    for copy in outward:
        copy.wait()


def factor(root_gram, sample, leaf):
    whole, hbm = pl.BlockSpec(memory_space=pltpu.VMEM), pl.BlockSpec(memory_space=pltpu.HBM)
    rows = pltpu.VMEM((PANEL * SUB, K), jnp.float32)
    return pl.pallas_call(
        factor_kernel,
        out_shape=(
            jax.ShapeDtypeStruct(sample.shape, sample.dtype),
            jax.ShapeDtypeStruct(leaf.shape, leaf.dtype),
            jax.ShapeDtypeStruct((1, K), jnp.float32),
        ),
        in_specs=[whole, hbm, hbm],
        out_specs=(hbm, hbm, whole),
        scratch_shapes=[
            pltpu.VMEM((1, K, 2 * K), jnp.float32),
            pltpu.VMEM((2 * K, K), jnp.float32),
            rows, rows,
            pltpu.VMEM(sample.shape, sample.dtype),
            pltpu.VMEM(leaf.shape, leaf.dtype),
            pltpu.SemaphoreType.DMA((4,)),
        ],
        name="factor",
    )(root_gram, sample, leaf)


def local(probe_matrix, near_blocks, block_cols):
    sample, leaf, root_gram = gather(block_cols, probe_matrix, near_blocks)
    return factor(root_gram, sample, leaf)


def solution(mesh):
    placed = (P("probe", "rows"), P("rows", "probe", None, None), P("rows", "probe"))
    return jax.shard_map(
        local,
        mesh=mesh,
        in_specs=placed,
        out_specs=(P("probe", "rows"), P("rows", "probe", None), P(("rows", "probe"), None)),
        check_vma=False,
    )
```

```python
import functools

import jax
import jax.numpy as jnp
from jax import lax
from jax.experimental import pallas as pl
from jax.experimental.pallas import tpu as pltpu
from jax.sharding import PartitionSpec as P

K = 128
LEAF = 256
PLANE = 16
PANEL = 16
BLOCK = 8
SUB = 8
HIGH = lax.Precision.HIGHEST
MESH = pl.DeviceIdType.MESH


def cross(a, b, precision=None):
    return lax.dot_general(
        a, b, (((1,), (1,)), ((), ())), precision=precision, preferred_element_type=jnp.float32
    )


def eliminate_block(rows, c0):
    e = {}
    for j in range(BLOCK):
        for i in range(j, BLOCK):
            e[j, i] = jnp.broadcast_to(rows[j][0][:, c0 + i:c0 + i + 1], (SUB, K))
    for j in range(BLOCK):
        rs = lax.rsqrt(e[j, j])
        f = {i: e[j, i] * rs for i in range(j + 1, BLOCK)}
        rows[j] = [h * rs for h in rows[j]]
        for i in range(j + 1, BLOCK):
            for i2 in range(i, BLOCK):
                e[i, i2] = e[i, i2] - f[i] * f[i2]
            rows[i] = [h - f[i] * p for h, p in zip(rows[i], rows[j])]
    for i in range(BLOCK, len(rows)):
        for j in range(BLOCK):
            f = jnp.broadcast_to(rows[j][0][:, c0 + i:c0 + i + 1], (SUB, K))
            rows[i] = [h - f * p for h, p in zip(rows[i], rows[j])]
    return rows


def factor_panel(a_ref, count, t0, t1, k):
    r0 = k * PANEL
    lane = lax.broadcasted_iota(jnp.int32, (PANEL, K), 1)
    sub = lax.broadcasted_iota(jnp.int32, (PANEL, K), 0)
    if count == 1:
        rows = [
            [jnp.broadcast_to(a_ref[0, r0 + r:r0 + r + 1, h * K:(h + 1) * K], (SUB, K)) for h in range(2)]
            for r in range(PANEL)
        ]
    else:
        for s in range(count):
            t0[pl.ds(s, PANEL, stride=SUB), :] = a_ref[s, r0:r0 + PANEL, 0:K]
            t1[pl.ds(s, PANEL, stride=SUB), :] = a_ref[s, r0:r0 + PANEL, K:2 * K]
        rows = [[t[SUB * r:SUB * r + SUB, :] for t in (t0, t1)] for r in range(PANEL)]
    for c in range(0, PANEL, BLOCK):
        rows = rows[:c] + eliminate_block(rows[c:], r0 + c)
    for r in range(PANEL):
        t0[SUB * r:SUB * r + SUB, :] = rows[r][0]
        t1[SUB * r:SUB * r + SUB, :] = rows[r][1]
    for s in range(count):
        low = jnp.where(lane >= r0 + sub, t0[pl.ds(s, PANEL, stride=SUB), :], 0.0)
        high = t1[pl.ds(s, PANEL, stride=SUB), :]
        a_ref[s, r0:r0 + PANEL, 0:K] = low
        a_ref[s, r0:r0 + PANEL, K:2 * K] = high
        if r0 + PANEL < K:
            left = low.T[r0 + PANEL:, :]
            right = jnp.concatenate([low, high], axis=1)
            a_ref[s, r0 + PANEL:, :] = a_ref[s, r0 + PANEL:, :] - jnp.dot(
                left, right, precision=HIGH, preferred_element_type=jnp.float32
            )


def gather_kernel(
    depth, cols_ref, probe_ref, blocks_ref,
    sample_ref, leaf_ref, root_ref,
    own, landing, window, blocks, given, kept, theirs, stage, sent_stage, total, rs_buf, z_buf,
    leaf_a, t0, t1, leaf_buf, sent_leaf,
    meet, block_sem, own_sem, share_send, share_recv, halo_send, halo_recv, pass_send, pass_recv,
    part_send, part_recv, tile_send, tile_recv, out_sem, leaf_send, leaf_recv, leaf_sem,
    rs_send, rs_recv, z_send, z_recv, ag_send, ag_recv,
):
    row, core = lax.axis_index("rows"), lax.axis_index("probe")
    rows = PLANE * depth
    sibling = (row, 1 - core)
    after, before = (lax.rem(row + 1, rows), core), (lax.rem(row + rows - 1, rows), core)
    layer, spot = row // PLANE, lax.rem(row, PLANE)
    side, front = lax.rem(spot, 4), spot // 4

    ring = [0, 1, 2, 1]
    plane_steps = sorted(
        [(dx, dy, o) for dx in range(4) for dy in range(4) for o in range(2) if dx or dy or o],
        key=lambda d: -ring[d[0]] - ring[d[1]],
    )
    column_steps = sorted(range(1, depth), key=lambda d: -min(d, depth - d))
    xs = [lax.rem(side + d, 4) for d in range(4)]
    ys = [lax.rem(front + d, 4) for d in range(4)]
    zs = [lax.rem(layer + d, depth) for d in range(depth)]
    spots = {(dx, dy): ys[dy] * 4 + xs[dx] for dx in range(4) for dy in range(4)}

    cores = (core, 1 - core)

    def in_plane(step):
        return (layer * PLANE + spots[step[:2]], cores[step[2]])

    def in_column(step):
        return (zs[step] * PLANE + spot, core)

    def opposite(step):
        return ((4 - step[0]) % 4, (4 - step[1]) % 4, step[2])

    def tile(step):
        return (
            pl.ds(pl.multiple_of(spots[step[:2]] * 8, 8), 8),
            pl.ds(pl.multiple_of(cores[step[2]] * K, K), K),
        )

    def slot(step):
        return (step[1] * 4 + step[0]) * 2 + step[2]

    along_x = [in_plane((d, 0, 0)) for d in (1, 3)]
    along_y = [in_plane((0, d, 0)) for d in (1, 3)]
    along_z = [in_column(d) for d in (1, depth - 1)]

    def greet(semaphore, targets):
        for target in targets:
            pl.semaphore_signal(semaphore, inc=1, device_id=target, device_id_type=MESH)

    def remote(src, dst, send, recv, target):
        return pltpu.make_async_remote_copy(
            src_ref=src, dst_ref=dst, send_sem=send, recv_sem=recv,
            device_id=target, device_id_type=MESH,
        )

    own_copies = {}
    for c in (7, 0, 6, 1, 5, 2, 4, 3):
        own_copies[c] = pltpu.make_async_copy(
            probe_ref.at[:, c * LEAF:(c + 1) * LEAF], own.at[core, c], own_sem.at[c]
        )
        own_copies[c].start()
    barrier = pltpu.get_barrier_semaphore()
    entered = [after, before, sibling] + along_x + along_y + along_z
    greet(barrier, entered)
    pl.semaphore_wait(barrier, len(entered))

    rounds = [
        ((meet.at[0], along_x), (meet.at[1], along_z)),
        ((meet.at[2], along_y), (meet.at[3], along_z)),
        ((meet.at[4], along_y), (meet.at[5], along_z)),
        ((meet.at[6], [sibling]),),
    ]

    def announce(n):
        for semaphore, targets in rounds[n]:
            greet(semaphore, targets)

    def learn(n):
        for semaphore, targets in rounds[n]:
            pl.semaphore_wait(semaphore, len(targets))

    halo = {}
    waited = set()
    for t in range(8):
        for which, c, target in ((0, 7 - t, after), (1, t, before)):
            if c not in waited:
                own_copies[c].wait()
                waited.add(c)
            halo[which, t] = remote(
                own.at[core, c], landing.at[which, c, core],
                halo_send.at[which, c], halo_recv.at[which, c], target,
            )
            halo[which, t].start()
    share = remote(own.at[core], own.at[core], share_send, share_recv, sibling)
    share.start()
    announce(0)

    def mine(n):
        return (1 - core) * (3 - n) + core * (4 + n)

    def block_copy(c):
        return pltpu.make_async_copy(blocks_ref.at[c], blocks.at[c], block_sem.at[c])

    for c in (3, 4, 2, 5, 1, 6, 0, 7):
        block_copy(c).start()
    share.wait_recv()
    for c in range(8):
        for half in range(2):
            window[8 + c, half * K:(half + 1) * K, :] = own[half, c]

    passed, parts, tiles = {}, {}, {}

    def absorb(t):
        for which, c in ((0, 7 - t), (1, t)):
            passed[which, t].wait_recv()
            for half in range(2):
                window[16 * which + c, half * K:(half + 1) * K, :] = landing[which, c, half]

    def product(c):
        acc = jnp.zeros((LEAF, LEAF), jnp.float32)
        for b in range(8):
            at = jnp.clip(cols_ref[c, b] - (row * 8 - 8), 0, 23)
            acc = acc + cross(window[at], blocks[c, b])
        return acc

    def multiply(n):
        block_copy(3 - n).wait()
        block_copy(4 + n).wait()
        given[n] = product(7 - mine(n))
        parts[n] = remote(given.at[n], theirs.at[n], part_send.at[n], part_recv.at[n], sibling)
        parts[n].start()
        kept[n] = product(mine(n))

    def sample_out(n, c):
        at = pl.multiple_of(c * LEAF, LEAF)
        return pltpu.make_async_copy(stage.at[c], sample_ref.at[:, pl.ds(at, LEAF)], out_sem.at[n])

    def finish(n):
        c = mine(n)
        parts[n].wait_recv()
        full = kept[n] + theirs[n]
        kept[n] = full
        gram = cross(full[:K], full, HIGH)
        leaf_a[n] = gram
        total[...] = gram if n == 0 else total[...] + gram

    def hand_out(n):
        c = mine(n)
        stage[c] = kept[n, pl.ds(pl.multiple_of(core * K, K), K), :].astype(jnp.bfloat16)
        sent_stage[n] = kept[n, pl.ds(pl.multiple_of((1 - core) * K, K), K), :].astype(jnp.bfloat16)
        tiles[n] = remote(sent_stage.at[n], stage.at[c], tile_send.at[n], tile_recv.at[n], sibling)
        tiles[n].start()
        sample_out(n, c).start()

    for t in range(9):
        if t < 8:
            for which, c in ((0, 7 - t), (1, t)):
                halo[which, t].wait_recv()
                passed[which, t] = remote(
                    landing.at[which, c, core], landing.at[which, c, core],
                    pass_send.at[which, c], pass_recv.at[which, c], sibling,
                )
                passed[which, t].start()
        if t >= 1:
            absorb(t - 1)
        if 1 <= t <= 4:
            learn(t - 1)
            if t < 4:
                announce(t)
        if t >= 5:
            multiply(t - 5)
        if 6 <= t < 7:
            finish(0)
    finish(1)
    finish(2)
    finish(3)

    here = tile((0, 0, 0))
    scatters = [
        remote(total.at[tile(step)], rs_buf.at[slot(step)], rs_send.at[slot(step)], rs_recv.at[slot(step)], in_plane(step))
        for step in plane_steps
    ]
    for copy in scatters:
        copy.start()
    rs_buf[0] = total[here]
    for n in range(4):
        hand_out(n)
    t0[...] = jnp.zeros_like(t0)
    t1[...] = jnp.zeros_like(t1)
    for k in range(0, 3):
        factor_panel(leaf_a, 4, t0, t1, k)
    for copy in scatters:
        copy.wait_recv()
    z_buf[0] = jnp.sum(rs_buf[...], axis=0)

    columns = [
        remote(z_buf.at[0], z_buf.at[step], z_send.at[step], z_recv.at[step], in_column(step))
        for step in column_steps
    ]
    for copy in columns:
        copy.start()
    for copy in scatters:
        copy.wait_send()
    for n in range(4):
        tiles[n].wait_recv()
        sample_out(4 + n, 7 - mine(n)).start()
    for k in range(3, 6):
        factor_panel(leaf_a, 4, t0, t1, k)
    for copy in columns:
        copy.wait_recv()
    root_ref[here] = jnp.sum(z_buf[...], axis=0)

    def publish(place, step):
        at = slot(step)
        return remote(root_ref.at[place], root_ref.at[place], ag_send.at[at], ag_recv.at[at], in_plane(step))

    published = [publish(here, step) for step in plane_steps]
    for copy in published:
        copy.start()
    for copy in columns:
        copy.wait_send()
    for k in range(6, 8):
        factor_panel(leaf_a, 4, t0, t1, k)
    leaves = []
    for n in range(4):
        sent_leaf[n] = leaf_a[n, :, pl.ds(pl.multiple_of((1 - core) * K, K), K)].T
        leaves.append(remote(sent_leaf.at[n], leaf_buf.at[mine(n)], leaf_send.at[n], leaf_recv.at[n], sibling))
        leaves[n].start()
        leaf_buf[mine(n)] = leaf_a[n, :, pl.ds(pl.multiple_of(core * K, K), K)].T
    for n in range(4):
        leaves[n].wait_recv()
    leaf_out = pltpu.make_async_copy(leaf_buf, leaf_ref, leaf_sem)
    leaf_out.start()
    for copy in published:
        copy.wait_send()
    for step in plane_steps:
        publish(tile(opposite(step)), step).wait_recv()
    share.wait_send()
    for copy in list(halo.values()) + list(passed.values()) + list(parts.values()) + list(tiles.values()) + leaves:
        copy.wait_send()
    for n in range(4):
        sample_out(n, mine(n)).wait()
        sample_out(4 + n, 7 - mine(n)).wait()
    leaf_out.wait()


def gather(block_cols, probe_matrix, near_blocks):
    depth = lax.axis_size("rows") // PLANE
    bf16, f32, dma = jnp.bfloat16, jnp.float32, pltpu.SemaphoreType.DMA
    hbm = pl.BlockSpec(memory_space=pltpu.HBM)
    return pl.pallas_call(
        functools.partial(gather_kernel, depth),
        out_shape=(
            jax.ShapeDtypeStruct((K, 8 * LEAF), bf16),
            jax.ShapeDtypeStruct((8, K, K), f32),
            jax.ShapeDtypeStruct((K, LEAF), f32),
        ),
        in_specs=[pl.BlockSpec(memory_space=pltpu.SMEM), hbm, hbm],
        out_specs=(hbm, hbm, pl.BlockSpec(memory_space=pltpu.VMEM)),
        scratch_shapes=[
            pltpu.VMEM((2, 8, K, LEAF), bf16),
            pltpu.VMEM((2, 8, 2, K, LEAF), bf16),
            pltpu.VMEM((24, LEAF, LEAF), bf16),
            pltpu.VMEM((8, 8, LEAF, LEAF), bf16),
            pltpu.VMEM((4, LEAF, LEAF), f32),
            pltpu.VMEM((4, LEAF, LEAF), f32),
            pltpu.VMEM((4, LEAF, LEAF), f32),
            pltpu.VMEM((8, K, LEAF), bf16),
            pltpu.VMEM((4, K, LEAF), bf16),
            pltpu.VMEM((K, LEAF), f32),
            pltpu.VMEM((2 * PLANE, 8, K), f32),
            pltpu.VMEM((depth, 8, K), f32),
            pltpu.VMEM((4, K, 2 * K), f32),
            pltpu.VMEM((PANEL * SUB, K), f32),
            pltpu.VMEM((PANEL * SUB, K), f32),
            pltpu.VMEM((8, K, K), f32),
            pltpu.VMEM((4, K, K), f32),
            pltpu.SemaphoreType.REGULAR((7,)),
            dma((8,)), dma((8,)), dma, dma, dma((2, 8)), dma((2, 8)), dma((2, 8)), dma((2, 8)),
            dma((4,)), dma((4,)), dma((4,)), dma((4,)), dma((8,)), dma((4,)), dma((4,)), dma,
            dma((2 * PLANE,)), dma((2 * PLANE,)), dma((depth,)), dma((depth,)), dma((2 * PLANE,)), dma((2 * PLANE,)),
        ],
        compiler_params=pltpu.CompilerParams(
            collective_id=0, has_side_effects=True, vmem_limit_bytes=56 * 2**20
        ),
        name="gather",
    )(block_cols, probe_matrix, near_blocks)


def factor_kernel(c_ref, sample_in, leaf_in, sample_ref, leaf_ref, out_ref, r_ref, f_ref, t0, t1, sample_v, leaf_v, sems):
    inward = [
        pltpu.make_async_copy(sample_in, sample_v, sems.at[0]),
        pltpu.make_async_copy(leaf_in, leaf_v, sems.at[1]),
    ]
    outward = [
        pltpu.make_async_copy(sample_v, sample_ref, sems.at[2]),
        pltpu.make_async_copy(leaf_v, leaf_ref, sems.at[3]),
    ]
    for copy in inward:
        copy.start()
    r_ref[0] = c_ref[...]
    for k in range(K // PANEL):
        factor_panel(r_ref, 1, t0, t1, k)
        if k == 3:
            for copy in inward:
                copy.wait()
            for copy in outward:
                copy.start()
    f_ref[...] = r_ref[0].T
    out_ref[...] = f_ref[pl.ds(lax.axis_index("rows") * 2 + lax.axis_index("probe"), 1), :]
    for copy in outward:
        copy.wait()


def factor(root_gram, sample, leaf):
    whole, hbm = pl.BlockSpec(memory_space=pltpu.VMEM), pl.BlockSpec(memory_space=pltpu.HBM)
    rows = pltpu.VMEM((PANEL * SUB, K), jnp.float32)
    return pl.pallas_call(
        factor_kernel,
        out_shape=(
            jax.ShapeDtypeStruct(sample.shape, sample.dtype),
            jax.ShapeDtypeStruct(leaf.shape, leaf.dtype),
            jax.ShapeDtypeStruct((1, K), jnp.float32),
        ),
        in_specs=[whole, hbm, hbm],
        out_specs=(hbm, hbm, whole),
        scratch_shapes=[
            pltpu.VMEM((1, K, 2 * K), jnp.float32),
            pltpu.VMEM((2 * K, K), jnp.float32),
            rows, rows,
            pltpu.VMEM(sample.shape, sample.dtype),
            pltpu.VMEM(leaf.shape, leaf.dtype),
            pltpu.SemaphoreType.DMA((4,)),
        ],
        name="factor",
    )(root_gram, sample, leaf)


def local(probe_matrix, near_blocks, block_cols):
    sample, leaf, root_gram = gather(block_cols, probe_matrix, near_blocks)
    return factor(root_gram, sample, leaf)


def solution(mesh):
    placed = (P("probe", "rows"), P("rows", "probe", None, None), P("rows", "probe"))
    return jax.shard_map(
        local,
        mesh=mesh,
        in_specs=placed,
        out_specs=(P("probe", "rows"), P("rows", "probe", None), P(("rows", "probe"), None)),
        check_vma=False,
    )
```

```python
import functools

import jax
import jax.numpy as jnp
from jax import lax
from jax.experimental import pallas as pl
from jax.experimental.pallas import tpu as pltpu
from jax.sharding import PartitionSpec as P

K = 128
LEAF = 256
PLANE = 16
PANEL = 16
BLOCK = 8
SUB = 8
HIGH = lax.Precision.HIGHEST
MESH = pl.DeviceIdType.MESH


def cross(a, b, precision=None):
    return lax.dot_general(
        a, b, (((1,), (1,)), ((), ())), precision=precision, preferred_element_type=jnp.float32
    )


def eliminate_block(rows, c0):
    e = {}
    for j in range(BLOCK):
        for i in range(j, BLOCK):
            e[j, i] = jnp.broadcast_to(rows[j][0][:, c0 + i:c0 + i + 1], (SUB, K))
    for j in range(BLOCK):
        rs = lax.rsqrt(e[j, j])
        f = {i: e[j, i] * rs for i in range(j + 1, BLOCK)}
        rows[j] = [h * rs for h in rows[j]]
        for i in range(j + 1, BLOCK):
            for i2 in range(i, BLOCK):
                e[i, i2] = e[i, i2] - f[i] * f[i2]
            rows[i] = [h - f[i] * p for h, p in zip(rows[i], rows[j])]
    for i in range(BLOCK, len(rows)):
        for j in range(BLOCK):
            f = jnp.broadcast_to(rows[j][0][:, c0 + i:c0 + i + 1], (SUB, K))
            rows[i] = [h - f * p for h, p in zip(rows[i], rows[j])]
    return rows


def factor_panel(a_ref, count, t0, t1, k):
    r0 = k * PANEL
    lane = lax.broadcasted_iota(jnp.int32, (PANEL, K), 1)
    sub = lax.broadcasted_iota(jnp.int32, (PANEL, K), 0)
    if count == 1:
        rows = [
            [jnp.broadcast_to(a_ref[0, r0 + r:r0 + r + 1, h * K:(h + 1) * K], (SUB, K)) for h in range(2)]
            for r in range(PANEL)
        ]
    else:
        for s in range(count):
            t0[pl.ds(s, PANEL, stride=SUB), :] = a_ref[s, r0:r0 + PANEL, 0:K]
            t1[pl.ds(s, PANEL, stride=SUB), :] = a_ref[s, r0:r0 + PANEL, K:2 * K]
        rows = [[t[SUB * r:SUB * r + SUB, :] for t in (t0, t1)] for r in range(PANEL)]
    for c in range(0, PANEL, BLOCK):
        rows = rows[:c] + eliminate_block(rows[c:], r0 + c)
    for r in range(PANEL):
        t0[SUB * r:SUB * r + SUB, :] = rows[r][0]
        t1[SUB * r:SUB * r + SUB, :] = rows[r][1]
    for s in range(count):
        low = jnp.where(lane >= r0 + sub, t0[pl.ds(s, PANEL, stride=SUB), :], 0.0)
        high = t1[pl.ds(s, PANEL, stride=SUB), :]
        a_ref[s, r0:r0 + PANEL, 0:K] = low
        a_ref[s, r0:r0 + PANEL, K:2 * K] = high
        if r0 + PANEL < K:
            left = low.T[r0 + PANEL:, :]
            right = jnp.concatenate([low, high], axis=1)
            a_ref[s, r0 + PANEL:, :] = a_ref[s, r0 + PANEL:, :] - jnp.dot(
                left, right, precision=HIGH, preferred_element_type=jnp.float32
            )


def gather_kernel(
    depth, cols_ref, probe_ref, blocks_ref,
    sample_ref, leaf_ref, root_ref,
    own, landing, window, blocks, given, kept, theirs, stage, sent_stage, total, rs_buf, z_buf,
    leaf_a, t0, t1, leaf_buf, sent_leaf,
    meet, block_sem, own_sem, share_send, share_recv, halo_send, halo_recv, pass_send, pass_recv,
    part_send, part_recv, tile_send, tile_recv, out_sem, leaf_send, leaf_recv, leaf_sem,
    rs_send, rs_recv, z_send, z_recv, ag_send, ag_recv,
):
    row, core = lax.axis_index("rows"), lax.axis_index("probe")
    rows = PLANE * depth
    sibling = (row, 1 - core)
    after, before = (lax.rem(row + 1, rows), core), (lax.rem(row + rows - 1, rows), core)
    layer, spot = row // PLANE, lax.rem(row, PLANE)
    side, front = lax.rem(spot, 4), spot // 4

    ring = [0, 1, 2, 1]
    plane_steps = sorted(
        [(dx, dy) for dx in range(4) for dy in range(4) if dx or dy], key=lambda d: -ring[d[0]] - ring[d[1]]
    )
    column_steps = sorted(
        [(dz, other) for dz in range(depth) for other in range(2) if dz or other],
        key=lambda d: -2 * min(d[0], depth - d[0]) - d[1],
    )
    xs = [lax.rem(side + d, 4) for d in range(4)]
    ys = [lax.rem(front + d, 4) for d in range(4)]
    zs = [lax.rem(layer + d, depth) for d in range(depth)]
    spots = {(dx, dy): ys[dy] * 4 + xs[dx] for dx in range(4) for dy in range(4)}

    def in_plane(step):
        return (layer * PLANE + spots[step], core)

    def in_column(step):
        return (zs[step[0]] * PLANE + spot, 1 - core if step[1] else core)

    def opposite(step):
        return ((4 - step[0]) % 4, (4 - step[1]) % 4)

    along_x = [in_plane((d, 0)) for d in (1, 3)]
    along_y = [in_plane((0, d)) for d in (1, 3)]
    along_z = [in_column((d, 0)) for d in (1, depth - 1)]

    def greet(semaphore, targets):
        for target in targets:
            pl.semaphore_signal(semaphore, inc=1, device_id=target, device_id_type=MESH)

    def remote(src, dst, send, recv, target):
        return pltpu.make_async_remote_copy(
            src_ref=src, dst_ref=dst, send_sem=send, recv_sem=recv,
            device_id=target, device_id_type=MESH,
        )

    own_copies = {}
    for c in (7, 0, 6, 1, 5, 2, 4, 3):
        own_copies[c] = pltpu.make_async_copy(
            probe_ref.at[:, c * LEAF:(c + 1) * LEAF], own.at[core, c], own_sem.at[c]
        )
        own_copies[c].start()
    root_ref[...] = jnp.zeros_like(root_ref)
    barrier = pltpu.get_barrier_semaphore()
    entered = [after, before, sibling] + along_x + along_y + along_z
    greet(barrier, entered)
    pl.semaphore_wait(barrier, len(entered))

    rounds = [
        ((meet.at[0], along_x), (meet.at[1], along_z)),
        ((meet.at[2], along_y), (meet.at[3], along_z)),
        ((meet.at[4], along_y), (meet.at[5], along_z)),
        ((meet.at[6], [sibling]),),
    ]

    def announce(n):
        for semaphore, targets in rounds[n]:
            greet(semaphore, targets)

    def learn(n):
        for semaphore, targets in rounds[n]:
            pl.semaphore_wait(semaphore, len(targets))

    halo = {}
    waited = set()
    for t in range(8):
        for which, c, target in ((0, 7 - t, after), (1, t, before)):
            if c not in waited:
                own_copies[c].wait()
                waited.add(c)
            halo[which, t] = remote(
                own.at[core, c], landing.at[which, c, core],
                halo_send.at[which, c], halo_recv.at[which, c], target,
            )
            halo[which, t].start()
    share = remote(own.at[core], own.at[core], share_send, share_recv, sibling)
    share.start()
    announce(0)

    def mine(n):
        return (1 - core) * (3 - n) + core * (4 + n)

    def block_copy(c):
        return pltpu.make_async_copy(blocks_ref.at[c], blocks.at[c], block_sem.at[c])

    for c in (3, 4, 2, 5, 1, 6, 0, 7):
        block_copy(c).start()
    share.wait_recv()
    for c in range(8):
        for half in range(2):
            window[8 + c, half * K:(half + 1) * K, :] = own[half, c]

    passed, parts, tiles = {}, {}, {}

    def absorb(t):
        for which, c in ((0, 7 - t), (1, t)):
            passed[which, t].wait_recv()
            for half in range(2):
                window[16 * which + c, half * K:(half + 1) * K, :] = landing[which, c, half]

    def product(c):
        acc = jnp.zeros((LEAF, LEAF), jnp.float32)
        for b in range(8):
            at = jnp.clip(cols_ref[c, b] - (row * 8 - 8), 0, 23)
            acc = acc + cross(window[at], blocks[c, b])
        return acc

    def multiply(n):
        block_copy(3 - n).wait()
        block_copy(4 + n).wait()
        given[n] = product(7 - mine(n))
        parts[n] = remote(given.at[n], theirs.at[n], part_send.at[n], part_recv.at[n], sibling)
        parts[n].start()
        kept[n] = product(mine(n))

    def sample_out(n, c):
        at = pl.multiple_of(c * LEAF, LEAF)
        return pltpu.make_async_copy(stage.at[c], sample_ref.at[:, pl.ds(at, LEAF)], out_sem.at[n])

    def finish(n):
        c = mine(n)
        parts[n].wait_recv()
        full = kept[n] + theirs[n]
        kept[n] = full
        gram = cross(full[:K], full, HIGH)
        leaf_a[n] = gram
        total[...] = gram if n == 0 else total[...] + gram

    def hand_out(n):
        c = mine(n)
        stage[c] = kept[n, pl.ds(pl.multiple_of(core * K, K), K), :].astype(jnp.bfloat16)
        sent_stage[n] = kept[n, pl.ds(pl.multiple_of((1 - core) * K, K), K), :].astype(jnp.bfloat16)
        tiles[n] = remote(sent_stage.at[n], stage.at[c], tile_send.at[n], tile_recv.at[n], sibling)
        tiles[n].start()
        sample_out(n, c).start()

    for t in range(9):
        if t < 8:
            for which, c in ((0, 7 - t), (1, t)):
                halo[which, t].wait_recv()
                passed[which, t] = remote(
                    landing.at[which, c, core], landing.at[which, c, core],
                    pass_send.at[which, c], pass_recv.at[which, c], sibling,
                )
                passed[which, t].start()
        if t >= 1:
            absorb(t - 1)
        if 1 <= t <= 4:
            learn(t - 1)
            if t < 4:
                announce(t)
        if t >= 5:
            multiply(t - 5)
        if 6 <= t < 7:
            finish(0)
    finish(1)
    finish(2)
    finish(3)

    here = pl.ds(pl.multiple_of(spot * 8, 8), 8)
    pieces = {step: pl.ds(pl.multiple_of(spots[step] * 8, 8), 8) for step in plane_steps}

    scatters = [
        remote(
            total.at[pieces[step], :], rs_buf.at[step[1] * 4 + step[0]],
            rs_send.at[step[1] * 4 + step[0]], rs_recv.at[step[1] * 4 + step[0]], in_plane(step),
        )
        for step in plane_steps
    ]
    for copy in scatters:
        copy.start()
    rs_buf[0] = total[here, :]
    for n in range(4):
        hand_out(n)
    t0[...] = jnp.zeros_like(t0)
    t1[...] = jnp.zeros_like(t1)
    for k in range(0, 3):
        factor_panel(leaf_a, 4, t0, t1, k)
    for copy in scatters:
        copy.wait_recv()
    z_buf[0] = jnp.sum(rs_buf[...], axis=0)

    columns = [
        remote(
            z_buf.at[0], z_buf.at[step[0] * 2 + step[1]],
            z_send.at[step[0] * 2 + step[1]], z_recv.at[step[0] * 2 + step[1]], in_column(step),
        )
        for step in column_steps
    ]
    for copy in columns:
        copy.start()
    for copy in scatters:
        copy.wait_send()
    for n in range(4):
        tiles[n].wait_recv()
        sample_out(4 + n, 7 - mine(n)).start()
    for k in range(3, 6):
        factor_panel(leaf_a, 4, t0, t1, k)
    for copy in columns:
        copy.wait_recv()
    root_ref[here, :] = jnp.sum(z_buf[...], axis=0)

    def publish(place, step, width):
        at = step[1] * 4 + step[0]
        part = root_ref.at[place, 0:width]
        return remote(part, part, ag_send.at[at], ag_recv.at[at], in_plane(step))

    upper = layer * (2 * PLANE) >= K
    widths = ((LEAF, upper), (K, jnp.logical_not(upper)))

    def start_publishing(width):
        for step in plane_steps:
            publish(here, step, width).start()

    def end_publishing(width):
        for step in plane_steps:
            publish(here, step, width).wait_send()
        for step in plane_steps:
            publish(pieces[opposite(step)], step, width).wait_recv()

    for width, when in widths:
        pl.when(when)(functools.partial(start_publishing, width))
    for copy in columns:
        copy.wait_send()
    for k in range(6, 8):
        factor_panel(leaf_a, 4, t0, t1, k)
    leaves = []
    for n in range(4):
        sent_leaf[n] = leaf_a[n, :, pl.ds(pl.multiple_of((1 - core) * K, K), K)].T
        leaves.append(remote(sent_leaf.at[n], leaf_buf.at[mine(n)], leaf_send.at[n], leaf_recv.at[n], sibling))
        leaves[n].start()
        leaf_buf[mine(n)] = leaf_a[n, :, pl.ds(pl.multiple_of(core * K, K), K)].T
    for n in range(4):
        leaves[n].wait_recv()
    leaf_out = pltpu.make_async_copy(leaf_buf, leaf_ref, leaf_sem)
    leaf_out.start()
    for width, when in widths:
        pl.when(when)(functools.partial(end_publishing, width))
    share.wait_send()
    for copy in list(halo.values()) + list(passed.values()) + list(parts.values()) + list(tiles.values()) + leaves:
        copy.wait_send()
    for n in range(4):
        sample_out(n, mine(n)).wait()
        sample_out(4 + n, 7 - mine(n)).wait()
    leaf_out.wait()


def gather(block_cols, probe_matrix, near_blocks):
    depth = lax.axis_size("rows") // PLANE
    bf16, f32, dma = jnp.bfloat16, jnp.float32, pltpu.SemaphoreType.DMA
    hbm = pl.BlockSpec(memory_space=pltpu.HBM)
    return pl.pallas_call(
        functools.partial(gather_kernel, depth),
        out_shape=(
            jax.ShapeDtypeStruct((K, 8 * LEAF), bf16),
            jax.ShapeDtypeStruct((8, K, K), f32),
            jax.ShapeDtypeStruct((K, LEAF), f32),
        ),
        in_specs=[pl.BlockSpec(memory_space=pltpu.SMEM), hbm, hbm],
        out_specs=(hbm, hbm, pl.BlockSpec(memory_space=pltpu.VMEM)),
        scratch_shapes=[
            pltpu.VMEM((2, 8, K, LEAF), bf16),
            pltpu.VMEM((2, 8, 2, K, LEAF), bf16),
            pltpu.VMEM((24, LEAF, LEAF), bf16),
            pltpu.VMEM((8, 8, LEAF, LEAF), bf16),
            pltpu.VMEM((4, LEAF, LEAF), f32),
            pltpu.VMEM((4, LEAF, LEAF), f32),
            pltpu.VMEM((4, LEAF, LEAF), f32),
            pltpu.VMEM((8, K, LEAF), bf16),
            pltpu.VMEM((4, K, LEAF), bf16),
            pltpu.VMEM((K, LEAF), f32),
            pltpu.VMEM((PLANE, 8, LEAF), f32),
            pltpu.VMEM((2 * depth, 8, LEAF), f32),
            pltpu.VMEM((4, K, 2 * K), f32),
            pltpu.VMEM((PANEL * SUB, K), f32),
            pltpu.VMEM((PANEL * SUB, K), f32),
            pltpu.VMEM((8, K, K), f32),
            pltpu.VMEM((4, K, K), f32),
            pltpu.SemaphoreType.REGULAR((7,)),
            dma((8,)), dma((8,)), dma, dma, dma((2, 8)), dma((2, 8)), dma((2, 8)), dma((2, 8)),
            dma((4,)), dma((4,)), dma((4,)), dma((4,)), dma((8,)), dma((4,)), dma((4,)), dma,
            dma((PLANE,)), dma((PLANE,)), dma((2 * depth,)), dma((2 * depth,)), dma((PLANE,)), dma((PLANE,)),
        ],
        compiler_params=pltpu.CompilerParams(
            collective_id=0, has_side_effects=True, vmem_limit_bytes=56 * 2**20
        ),
        name="gather",
    )(block_cols, probe_matrix, near_blocks)


def factor_kernel(c_ref, sample_in, leaf_in, sample_ref, leaf_ref, out_ref, r_ref, f_ref, t0, t1, sample_v, leaf_v, sems):
    inward = [
        pltpu.make_async_copy(sample_in, sample_v, sems.at[0]),
        pltpu.make_async_copy(leaf_in, leaf_v, sems.at[1]),
    ]
    outward = [
        pltpu.make_async_copy(sample_v, sample_ref, sems.at[2]),
        pltpu.make_async_copy(leaf_v, leaf_ref, sems.at[3]),
    ]
    for copy in inward:
        copy.start()
    r_ref[0] = c_ref[...]
    for k in range(K // PANEL):
        factor_panel(r_ref, 1, t0, t1, k)
        if k == 3:
            for copy in inward:
                copy.wait()
            for copy in outward:
                copy.start()
    f_ref[...] = r_ref[0].T
    out_ref[...] = f_ref[pl.ds(lax.axis_index("rows") * 2 + lax.axis_index("probe"), 1), :]
    for copy in outward:
        copy.wait()


def factor(root_gram, sample, leaf):
    whole, hbm = pl.BlockSpec(memory_space=pltpu.VMEM), pl.BlockSpec(memory_space=pltpu.HBM)
    rows = pltpu.VMEM((PANEL * SUB, K), jnp.float32)
    return pl.pallas_call(
        factor_kernel,
        out_shape=(
            jax.ShapeDtypeStruct(sample.shape, sample.dtype),
            jax.ShapeDtypeStruct(leaf.shape, leaf.dtype),
            jax.ShapeDtypeStruct((1, K), jnp.float32),
        ),
        in_specs=[whole, hbm, hbm],
        out_specs=(hbm, hbm, whole),
        scratch_shapes=[
            pltpu.VMEM((1, K, 2 * K), jnp.float32),
            pltpu.VMEM((2 * K, K), jnp.float32),
            rows, rows,
            pltpu.VMEM(sample.shape, sample.dtype),
            pltpu.VMEM(leaf.shape, leaf.dtype),
            pltpu.SemaphoreType.DMA((4,)),
        ],
        name="factor",
    )(root_gram, sample, leaf)


def local(probe_matrix, near_blocks, block_cols):
    sample, leaf, root_gram = gather(block_cols, probe_matrix, near_blocks)
    return factor(root_gram, sample, leaf)


def solution(mesh):
    placed = (P("probe", "rows"), P("rows", "probe", None, None), P("rows", "probe"))
    return jax.shard_map(
        local,
        mesh=mesh,
        in_specs=placed,
        out_specs=(P("probe", "rows"), P("rows", "probe", None), P(("rows", "probe"), None)),
        check_vma=False,
    )
```
